32 devices in a mesh: enc: 2 (over x), row: 4 (over y, core), col: 4 (over z).
Axes of the slice: x: 2, y: 2, z: 4, core: 2. Of those that a mesh axis runs over, the one named last changes fastest.
Arguments:
- queries: bfloat16 [2560, 3072], P(('row', 'col'), 'enc'), may hold values from -150 to 150
- self_keys: bfloat16 [2560, 3072], P(('row', 'col'), 'enc'), may hold values from -150 to 150
- self_values: bfloat16 [2560, 3072], P(('row', 'col'), 'enc'), may hold values from -6 to 6
- positions: int32 [2560, 3], P(('row', 'col')), may hold values from 0 to 31, as said below
- query_gain: float32 [3072], P('enc'), may hold values from 1.3 to 2
- key_gain: float32 [3072], P('enc'), may hold values from 1.3 to 2
- context_keys: bfloat16 [32, 3072], P(('enc', 'row')), may hold values from -150 to 150
- context_values: bfloat16 [32, 3072], P(('enc', 'row')), may hold values from -6 to 6
- context_gain: float32 [3072], replicated, may hold values from 0.1 to 1.9
- image_cotangent: bfloat16 [2560, 3072], P(('row', 'col'), 'enc'), may hold values from -6 to 6
Outputs:
- self_mixed: bfloat16 [2560, 3072], P(('row', 'col'), 'enc')
- image_mixed: bfloat16 [2560, 3072], P(('row', 'col'), 'enc')
- grad_context_keys: float32 [32, 3072], P(('enc', 'row'))
- grad_context_values: float32 [32, 3072], P(('enc', 'row'))
The draws below stay inside these ranges and needn't reach their ends.
Inputs may be any that keep to these rules, and one draw needn't show every extreme that they name: `positions`: each (frame, patch row, patch column) of the 5 x 32 x 16 grid appears once; the tokens of one device form one tile of 8 x 4 patches in every frame, in order of frame, row, column; which tile lies on which device is drawn.
All inputs are finite; a program needn't handle non-finite values.
Results may differ from the reference program's by a relative error of at most 0.002.
The reference program's roundings to bfloat16 on the way (of `query_turned`, `key_turned`, `weights`, `query_plain`, `context_normed`, `probs_low` and `grad_scores`) count: a program that leaves them out, or rounds other values in their place, can miss the bound.
Values may be sent and summed in bfloat16 or wider, within the bound.
No kernel may reach another device: no remote copies, remote signals or barrier semaphores. Data moves between devices by JAX's collectives and lax.ppermute only.
A program may use at most 128 MiB of HBM per device.

```python
import math
import jax
import jax.numpy as jnp
from jax import lax

HEADS = 24
HEAD_DIM = 128
TILE_H = 8
TILE_W = 4
WIDTH = 3072
GH = 32
GW = 16
TILE = 160
TOKENS = 2560
CTX = 32


def feature_scales(key, falling):
    head_rank = (jnp.arange(WIDTH) // HEAD_DIM).astype(jnp.float32)
    share = head_rank / max(HEADS - 1, 1)
    if falling:
        share = 1.0 - share
    ramped = 2.0 ** share
    rough = jnp.exp(jax.random.uniform(key, (WIDTH,)) * math.log(10.0))
    return ramped * rough


def rough_rows(key, row_count, falling):
    base = jax.random.normal(jax.random.fold_in(key, 1), (row_count, WIDTH))
    row_scale = jnp.exp(jax.random.uniform(jax.random.fold_in(key, 2), (row_count, 1)) * math.log(10.0))
    return base * row_scale * feature_scales(jax.random.fold_in(key, 3), falling) / 10.0


def draw_queries(key, part):
    drawn = rough_rows(jax.random.fold_in(key, 101), TOKENS, False)
    return jnp.clip(drawn, -150.0, 150.0).astype(jnp.bfloat16)


def draw_self_keys(key, part):
    drawn = rough_rows(jax.random.fold_in(key, 202), TOKENS, True)
    return jnp.clip(drawn, -150.0, 150.0).astype(jnp.bfloat16)


def draw_context_keys(key, part):
    drawn = rough_rows(jax.random.fold_in(key, 303), CTX, False)
    return jnp.clip(drawn, -150.0, 150.0).astype(jnp.bfloat16)


def draw_positions(key, part):
    tiles_down = GH // TILE_H
    tiles_across = GW // TILE_W
    tile_count = tiles_down * tiles_across
    order = jax.random.permutation(jax.random.fold_in(key, 7), tile_count)
    local = jnp.arange(TILE)
    frame = local // (TILE_H * TILE_W)
    down = local // TILE_W % TILE_H
    across = local % TILE_W
    tile_row = order // tiles_across
    tile_col = order % tiles_across
    coords = jnp.stack([jnp.broadcast_to(frame[None, :], (tile_count, TILE)), tile_row[:, None] * TILE_H + down[None, :], tile_col[:, None] * TILE_W + across[None, :]], axis=-1)
    return coords.reshape(TOKENS, 3).astype(jnp.int32)


def level_of(rng, shape, split, low, top_value):
    factor_of = 1.0
    for dim, shards_of in split:
        heights = jax.random.uniform(jax.random.fold_in(jax.random.fold_in(rng, 6), dim), (shards_of,), jnp.float32, low / len(split), top_value / len(split))
        factor_of = factor_of * jnp.repeat(jnp.exp(heights), shape[dim] // shards_of).reshape((-1,) + (1,) * (len(shape) - 1 - dim))
    return factor_of


def centred(own_key, extent, width, reach, split=(), held_as=jnp.bfloat16):
    level = level_of(own_key, extent, split, -0.22, 0.18) if split else 1.0
    array = jax.random.normal(own_key, extent, jnp.float32) * width * level
    return jnp.minimum(jnp.maximum(array, -reach), reach).astype(held_as)


def setup_inputs(seed: int = 0) -> dict:
    key_of = jax.random.split(jax.random.key(seed), 11)
    queries = draw_queries(jax.random.fold_in(key_of[10], 71), 0)
    self_keys = draw_self_keys(jax.random.fold_in(key_of[10], 71), 0)
    self_values = centred(key_of[2], (TOKENS, WIDTH), 1.0, 6.0, ((0, 16), (1, 2)))
    positions = draw_positions(jax.random.fold_in(key_of[10], 71), 0)
    query_gain = jnp.clip(jnp.exp(math.log(2.0) - 0.43078295 * jax.random.uniform(key_of[4], (WIDTH,), jnp.float32) ** level_of(key_of[4], (WIDTH,), ((0, 2),), -0.2, 0.2)), 1.3, 2.0)
    key_gain = jnp.clip(jnp.exp(math.log(2.0) - 0.43078295 * jax.random.uniform(key_of[5], (WIDTH,), jnp.float32) ** level_of(key_of[5], (WIDTH,), ((0, 2),), -0.2, 0.2)), 1.3, 2.0)
    context_keys = draw_context_keys(jax.random.fold_in(key_of[10], 71), 0)
    context_values = centred(key_of[7], (CTX, WIDTH), 1.0, 6.0, ((0, 8),))
    context_gain = jnp.clip(1.0 + 0.18 * jax.random.normal(key_of[8], (WIDTH,), jnp.float32), 0.1, 1.9)
    image_cotangent = centred(key_of[9], (TOKENS, WIDTH), 1.0, 6.0, ((0, 16), (1, 2)))
    return dict(queries=queries, self_keys=self_keys, self_values=self_values, positions=positions, query_gain=query_gain, key_gain=key_gain, context_keys=context_keys, context_values=context_values, context_gain=context_gain, image_cotangent=image_cotangent)


eps = 1e-06

def rope_angles(positions):
    half = HEAD_DIM // 2
    part_side = HEAD_DIM // 6
    part_time = half - 2 * part_side
    freq_time = 1.0 / 10000.0 ** (jnp.arange(part_time, dtype=jnp.float32) * 2.0 / (2 * part_time))
    freq_side = 1.0 / 10000.0 ** (jnp.arange(part_side, dtype=jnp.float32) * 2.0 / (2 * part_side))
    zeros_side = jnp.zeros((part_side,), jnp.float32)
    zeros_time = jnp.zeros((part_time,), jnp.float32)
    time_row = jnp.concatenate([freq_time, zeros_side, zeros_side])
    height_row = jnp.concatenate([zeros_time, freq_side, zeros_side])
    width_row = jnp.concatenate([zeros_time, zeros_side, freq_side])
    coords = positions.astype(jnp.float32)
    return coords[:, 0:1] * time_row + coords[:, 1:2] * height_row + coords[:, 2:3] * width_row

def rms_normed(wide, gain):
    return wide * lax.rsqrt(lax.optimization_barrier(jnp.mean(wide * wide, axis=1, keepdims=True)) + eps) * gain

def rotate(normed, angles):
    row_count = normed.shape[0]
    half = HEAD_DIM // 2
    pairs = normed.reshape(row_count, HEADS, half, 2)
    even_part = pairs[..., 0]
    odd_part = pairs[..., 1]
    cosine = jnp.cos(angles)[:, None, :]
    sine = jnp.sin(angles)[:, None, :]
    turned = jnp.stack([even_part * cosine - odd_part * sine, even_part * sine + odd_part * cosine], axis=-1)
    return turned.reshape(row_count, HEADS * HEAD_DIM)

def rounded(wide):
    return lax.optimization_barrier(wide.astype(jnp.bfloat16)).astype(jnp.float32)

def by_heads(matrix, row_count):
    return matrix.reshape(row_count, HEADS, HEAD_DIM).transpose(1, 0, 2).astype(jnp.float32)

def self_attention(query_turned, key_turned, self_values, score_scale):
    block = math.gcd(TOKENS, 512)
    query_heads = by_heads(query_turned, TOKENS)
    key_heads = by_heads(key_turned, TOKENS)
    value_heads = by_heads(self_values, TOKENS)

    def one_head(operands):
        query_head, key_head, value_head = operands

        def one_block(query_block):
            scores = jnp.dot(query_block, key_head.T, precision=lax.Precision.HIGHEST) * score_scale
            peak = lax.optimization_barrier(jnp.max(scores, axis=1, keepdims=True))
            weights = jnp.exp(scores - peak)
            weight_sum = lax.optimization_barrier(jnp.sum(weights, axis=1, keepdims=True))
            mixed = jnp.dot(rounded(weights), value_head, precision=lax.Precision.HIGHEST)
            return mixed / weight_sum
        outcome = lax.map(one_block, query_head.reshape(TOKENS // block, block, HEAD_DIM))
        return outcome.reshape(TOKENS, HEAD_DIM)
    mixed = lax.map(one_head, (query_heads, key_heads, value_heads))
    return mixed.transpose(1, 0, 2).reshape(TOKENS, HEADS * HEAD_DIM).astype(jnp.bfloat16)

def cross_attention(query_plain, context_normed, context_values, image_cotangent, score_scale):
    query_heads = by_heads(query_plain, TOKENS)
    key_heads = by_heads(context_normed, CTX)
    value_heads = by_heads(context_values, CTX)
    cotangent_heads = by_heads(image_cotangent, TOKENS)

    def one_head(operands):
        query_head, key_head, value_head, cotangent_head = operands
        scores = jnp.dot(query_head, key_head.T, precision=lax.Precision.HIGHEST) * score_scale
        peak = lax.optimization_barrier(jnp.max(scores, axis=1, keepdims=True))
        weights = jnp.exp(scores - peak)
        probs = weights / lax.optimization_barrier(jnp.sum(weights, axis=1, keepdims=True))
        probs_low = rounded(probs)
        mixed = jnp.dot(probs_low, value_head, precision=lax.Precision.HIGHEST)
        grad_values = jnp.dot(probs_low.T, cotangent_head, precision=lax.Precision.HIGHEST)
        grad_probs = jnp.dot(cotangent_head, value_head.T, precision=lax.Precision.HIGHEST)
        inner = lax.optimization_barrier(jnp.sum(probs * grad_probs, axis=1, keepdims=True))
        grad_scores = rounded(probs * (grad_probs - inner))
        grad_keys = jnp.dot(grad_scores.T, query_head, precision=lax.Precision.HIGHEST) * score_scale
        return (mixed, grad_keys, grad_values)
    mixed, grad_keys, grad_values = lax.map(one_head, (query_heads, key_heads, value_heads, cotangent_heads))
    image_out = mixed.transpose(1, 0, 2).reshape(TOKENS, HEADS * HEAD_DIM).astype(jnp.bfloat16)
    grad_keys = grad_keys.transpose(1, 0, 2).reshape(CTX, HEADS * HEAD_DIM)
    grad_values = grad_values.transpose(1, 0, 2).reshape(CTX, HEADS * HEAD_DIM)
    return (image_out, grad_keys, grad_values)

def reference(queries, self_keys, self_values, positions, query_gain, key_gain, context_keys, context_values, context_gain, image_cotangent):
    score_scale = HEAD_DIM ** (-0.5)
    query_normed = rms_normed(queries.astype(jnp.float32), query_gain)
    key_normed = rms_normed(self_keys.astype(jnp.float32), key_gain)
    angles = rope_angles(positions)
    query_turned = rotate(query_normed, angles).astype(jnp.bfloat16)
    key_turned = rotate(key_normed, angles).astype(jnp.bfloat16)
    self_out = self_attention(query_turned, key_turned, self_values, score_scale)
    query_plain = query_normed.astype(jnp.bfloat16)
    context_wide = context_keys.astype(jnp.float32)
    context_recip = lax.rsqrt(lax.optimization_barrier(jnp.mean(context_wide * context_wide, axis=1, keepdims=True)) + eps)
    context_normed = (context_wide * context_recip * context_gain).astype(jnp.bfloat16)
    image_out, grad_normed, grad_values = cross_attention(query_plain, context_normed, context_values, image_cotangent, score_scale)
    scaled_grad = context_gain * grad_normed
    grad_keys = context_recip * scaled_grad - context_wide * context_recip ** 3 * lax.optimization_barrier(jnp.mean(context_wide * scaled_grad, axis=1, keepdims=True))
    return (self_out, image_out, grad_keys, grad_values)
```

```python
import functools

import jax
import jax.numpy as jnp
import numpy as np
from jax import lax
from jax.experimental import pallas as pl
from jax.experimental.pallas import tpu as pltpu
from jax.sharding import PartitionSpec as P

HEAD_DIM = 128
eps = 1e-06
LOG2E = 1.4426950408889634
NT = (((1,), (1,)), ((), ()))
TN = (((0,), (0,)), ((), ()))
VMEM_LIMIT = 48 * 1024 * 1024


def swap(x, axis, size, k):
    return lax.ppermute(x, axis, [(i, i ^ k) for i in range(size)])


def kernel_call(body, out_shape, cost=(0, 0, 0), **kw):
    return pl.pallas_call(
        body,
        out_shape=out_shape,
        compiler_params=pltpu.CompilerParams(vmem_limit_bytes=VMEM_LIMIT),
        cost_estimate=pl.CostEstimate(flops=cost[0], bytes_accessed=cost[1], transcendentals=cost[2]),
        **kw,
    )


def rope_tables(positions):
    half = HEAD_DIM // 2
    part_side = HEAD_DIM // 6
    part_time = half - 2 * part_side
    freq_time = 1.0 / 10000.0 ** (jnp.arange(part_time, dtype=jnp.float32) * 2.0 / (2 * part_time))
    freq_side = 1.0 / 10000.0 ** (jnp.arange(part_side, dtype=jnp.float32) * 2.0 / (2 * part_side))
    freq = jnp.repeat(jnp.concatenate([freq_time, freq_side, freq_side]), 2)
    pair = np.arange(HEAD_DIM) // 2
    coords = positions.astype(jnp.float32)
    coord = jnp.where(
        pair < part_time,
        coords[:, 0:1],
        jnp.where(pair < part_time + part_side, coords[:, 1:2], coords[:, 2:3]),
    )
    angles = coord * freq
    sign = np.where(np.arange(HEAD_DIM) % 2 == 0, -1.0, 1.0).astype(np.float32)
    return jnp.cos(angles), jnp.sin(angles) * sign


def columns_of(axis, k, width):
    start = (lax.axis_index(axis) ^ k) * width
    return pl.ds(pl.multiple_of(start, HEAD_DIM), width)


def split_columns(x, axis, parts):
    rows, width = x.shape
    piece = width // parts

    def body(x_ref, *outs):
        for k in range(parts):
            outs[k][...] = x_ref[:, columns_of(axis, k, piece)]

    return kernel_call(
        body,
        [jax.ShapeDtypeStruct((rows, piece), x.dtype)] * parts,
        (0, 4 * rows * width, 0),
    )(x)


def join_columns(pieces, axis):
    rows, piece = pieces[0].shape
    parts = len(pieces)

    def body(*refs):
        for k in range(parts):
            refs[parts][:, columns_of(axis, k, piece)] = refs[k][...]

    return kernel_call(
        body,
        jax.ShapeDtypeStruct((rows, piece * parts), pieces[0].dtype),
        (0, 4 * rows * piece * parts, 0),
    )(*pieces)


def square_sums(queries, keys):
    rows, width = queries.shape

    def body(q_ref, k_ref, out_ref):
        for i, ref in enumerate((q_ref, k_ref)):
            wide = ref[...].astype(jnp.float32)
            out_ref[:, i : i + 1] = jnp.sum(wide * wide, axis=1, keepdims=True)

    return kernel_call(
        body, jax.ShapeDtypeStruct((rows, 2), jnp.float32), (4 * rows * width, 4 * rows * width, 0)
    )(queries, keys)


def normed_turned(x, which, totals, gain, cosine, sine, full_width, axis, parts, plain):
    rows, width = x.shape
    piece = width // parts
    n_totals = len(totals)

    def body(*refs):
        total_refs = refs[:n_totals]
        x_ref, gain_ref, cos_ref, sin_ref = refs[n_totals : n_totals + 4]
        outs = refs[n_totals + 4 :]
        total = total_refs[0][:, which : which + 1]
        for ref in total_refs[1:]:
            total = total + ref[:, which : which + 1]
        recip = lax.rsqrt(total / full_width + eps)
        cos = cos_ref[...]
        sin = sin_ref[...]
        even = lax.broadcasted_iota(jnp.int32, cos.shape, 1) % 2 == 0
        for k in range(parts):
            for h in range(piece // HEAD_DIM):
                start = (lax.axis_index(axis) ^ k) * piece + h * HEAD_DIM if parts > 1 else h * HEAD_DIM
                cols = pl.ds(pl.multiple_of(start, HEAD_DIM), HEAD_DIM)
                normed = x_ref[:, cols].astype(jnp.float32) * recip * gain_ref[:, cols]
                if plain:
                    outs[parts][:, cols] = normed.astype(jnp.bfloat16)
                other = jnp.where(
                    even, pltpu.roll(normed, HEAD_DIM - 1, 1), pltpu.roll(normed, 1, 1)
                )
                outs[k][:, h * HEAD_DIM : (h + 1) * HEAD_DIM] = (normed * cos + other * sin).astype(
                    jnp.bfloat16
                )

    shapes = [jax.ShapeDtypeStruct((rows, piece), jnp.bfloat16)] * parts
    if plain:
        shapes = shapes + [jax.ShapeDtypeStruct((rows, width), jnp.bfloat16)]
    return kernel_call(body, shapes, (10 * rows * width, 4 * rows * width, 0))(
        *totals, x, gain[None, :], cosine, sine
    )


def attention(query, keys, values):
    rows, width = query.shape
    heads = width // HEAD_DIM
    n = len(keys)
    total = sum(k.shape[0] for k in keys)
    factor = HEAD_DIM ** (-0.5) * LOG2E

    def body(q_ref, *refs):
        out_ref = refs[2 * n]
        q = q_ref[...]
        scores = [
            lax.dot_general(q, k[...], NT, preferred_element_type=jnp.float32) for k in refs[:n]
        ]
        peak = functools.reduce(
            jnp.maximum, [jnp.max(s, axis=1, keepdims=True) for s in scores]
        )
        weight_sum = 0.0
        mixed = 0.0
        for s, v in zip(scores, refs[n : 2 * n]):
            weights = jnp.exp2((s - peak) * factor)
            weight_sum = weight_sum + jnp.sum(weights, axis=1, keepdims=True)
            mixed = mixed + jnp.dot(
                weights.astype(jnp.bfloat16), v[...], preferred_element_type=jnp.float32
            )
        out_ref[...] = (mixed / weight_sum).astype(jnp.bfloat16)

    def spec(x):
        return pl.BlockSpec((x.shape[0], HEAD_DIM), lambda h: (0, h))

    return kernel_call(
        body,
        jax.ShapeDtypeStruct((rows, width), jnp.bfloat16),
        (4 * rows * total * width, 4 * total * width, rows * total * heads),
        grid=(heads,),
        in_specs=[spec(query)] + [spec(x) for x in keys] + [spec(x) for x in values],
        out_specs=spec(query),
    )(query, *keys, *values)


def image_attention(query_plain, context, cotangent):
    rows, width = query_plain.shape
    count = context.shape[1]
    heads = width // HEAD_DIM
    half = count // 2
    scale = HEAD_DIM ** (-0.5)

    def body(q_ref, c_ref, g_ref, out_ref, keep_ref, send_ref):
        for h in range(heads):
            cols = slice(h * HEAD_DIM, (h + 1) * HEAD_DIM)
            q = q_ref[:, cols]
            g = g_ref[:, cols]
            k = c_ref[0, :, cols]
            v = c_ref[1, :, cols]
            scores = lax.dot_general(k, q, NT, preferred_element_type=jnp.float32) * scale
            weights = jnp.exp(scores - jnp.max(scores, axis=0, keepdims=True))
            probs = weights / jnp.sum(weights, axis=0, keepdims=True)
            low = probs.astype(jnp.bfloat16)
            out_ref[:, cols] = lax.dot_general(
                low, v, TN, preferred_element_type=jnp.float32
            ).astype(jnp.bfloat16)
            grad_v = jnp.dot(low, g, preferred_element_type=jnp.float32)
            grad_p = lax.dot_general(v, g, NT, preferred_element_type=jnp.float32)
            inner = jnp.sum(probs * grad_p, axis=0, keepdims=True)
            grad_s = (probs * (grad_p - inner)).astype(jnp.bfloat16)
            grad_k = jnp.dot(grad_s, q, preferred_element_type=jnp.float32) * scale
            for i, grad in enumerate((grad_k, grad_v)):
                keep_ref[i, :, cols] = grad[:half]
                send_ref[i, :, cols] = grad[half:]

    return kernel_call(
        body,
        [
            jax.ShapeDtypeStruct((rows, width), jnp.bfloat16),
            jax.ShapeDtypeStruct((2, half, width), jnp.float32),
            jax.ShapeDtypeStruct((2, half, width), jnp.float32),
        ],
        (10 * rows * count * width, 8 * rows * width, rows * count * heads),
    )(query_plain, context, cotangent)


def per_device(
    sizes,
    queries,
    self_keys,
    self_values,
    positions,
    query_gain,
    key_gain,
    context_keys,
    context_values,
    context_gain,
    image_cotangent,
):
    n_enc, n_row, n_col = sizes
    rows, width = queries.shape
    heads = width // HEAD_DIM
    full_width = width * n_enc
    parts = n_col if heads % n_col == 0 else 1
    enc_index = lax.axis_index("enc")

    def exchange(pieces):
        return [pieces[0]] + [swap(pieces[k], "col", n_col, k) for k in range(1, parts)]

    def spread(pieces):
        if parts == 1:
            return [lax.all_gather(pieces[0], ("row", "col"), axis=0, tiled=True)]
        held = [jnp.concatenate(pieces, axis=0)]
        bit = n_row // 2
        while bit:
            held = held + [swap(x, "row", n_row, bit) for x in held]
            bit //= 2
        return held

    value_pieces = exchange(split_columns(self_values, "col", parts))

    sums = square_sums(queries, self_keys)
    totals = [sums]
    bit = 1
    while bit < n_enc:
        if len(totals) > 1:
            totals = [totals[0] + totals[1]]
        totals = [totals[0], swap(totals[0], "enc", n_enc, bit)]
        bit *= 2
    cosine, sine = rope_tables(positions)

    context_wide = context_keys.astype(jnp.float32)
    context_recip = lax.rsqrt(jnp.mean(context_wide * context_wide, axis=1, keepdims=True) + eps)
    context_normed = (context_wide * context_recip * context_gain).astype(jnp.bfloat16)
    own_count = context_keys.shape[0]
    context_both = jnp.stack([context_normed, context_values])
    context = []
    for k in range(n_enc):
        piece = lax.dynamic_slice_in_dim(context_both, (enc_index ^ k) * width, width, axis=2)
        context.append(swap(piece, "enc", n_enc, k) if k else piece)
    context = jnp.concatenate(context, axis=1)
    bit = n_row // 2
    while bit:
        context = jnp.concatenate([context, swap(context, "row", n_row, bit)], axis=1)
        bit //= 2

    key_pieces = normed_turned(
        self_keys, 1, totals, key_gain, cosine, sine, full_width, "col", parts, False
    )
    key_pieces = exchange(key_pieces)
    *query_pieces, query_plain = normed_turned(
        queries, 0, totals, query_gain, cosine, sine, full_width, "col", parts, True
    )
    query_pieces = exchange(query_pieces)

    image_out, grad, sent = image_attention(query_plain, context, image_cotangent)

    all_values = spread(value_pieces)
    all_keys = spread(key_pieces)

    bit = 1
    while bit < n_row:
        grad = grad + swap(sent, "row", n_row, bit)
        bit *= 2
        if bit < n_row:
            half = grad.shape[1] // 2
            grad, sent = grad[:, :half], grad[:, half:]
    bit = n_col // 2
    while bit:
        grad = grad + swap(grad, "col", n_col, bit)
        bit //= 2
    grad = grad.reshape(2, n_enc, own_count, width)
    grad = jnp.stack([grad[:, 0]] + [swap(grad[:, k], "enc", n_enc, k) for k in range(1, n_enc)])
    grad = jnp.concatenate(
        [lax.dynamic_index_in_dim(grad, enc_index ^ k, 0, False) for k in range(n_enc)], axis=2
    )
    scaled_grad = context_gain * grad[0]
    grad_keys_in = context_recip * scaled_grad - context_wide * context_recip**3 * jnp.mean(
        context_wide * scaled_grad, axis=1, keepdims=True
    )

    mixed = [None] * parts
    for k in reversed(range(parts)):
        piece = attention(query_pieces[k], all_keys, all_values)
        mixed[k] = swap(piece, "col", n_col, k) if k else piece
    self_out = join_columns(mixed, "col") if parts > 1 else mixed[0]

    return (self_out, image_out, grad_keys_in, grad[1])


def solution(mesh):
    sizes = tuple(mesh.shape[a] for a in ("enc", "row", "col"))
    return jax.shard_map(
        functools.partial(per_device, sizes),
        mesh=mesh,
        in_specs=(
            P(("row", "col"), "enc"),
            P(("row", "col"), "enc"),
            P(("row", "col"), "enc"),
            P(("row", "col"), None),
            P("enc"),
            P("enc"),
            P(("enc", "row"), None),
            P(("enc", "row"), None),
            P(),
            P(("row", "col"), "enc"),
        ),
        out_specs=(
            P(("row", "col"), "enc"),
            P(("row", "col"), "enc"),
            P(("enc", "row"), None),
            P(("enc", "row"), None),
        ),
        check_vma=False,
    )
```

```python
import functools
import math

import jax
import jax.numpy as jnp
import numpy as np
from jax import lax
from jax.experimental import pallas as pl
from jax.experimental.pallas import tpu as pltpu
from jax.sharding import PartitionSpec as P

HEAD_DIM = 128
eps = 1e-06
LOG2E = 1.4426950408889634
NT = (((1,), (1,)), ((), ()))
TN = (((0,), (0,)), ((), ()))
VMEM_LIMIT = 20 * 1024 * 1024


def swap(x, axis, size, k):
    return lax.ppermute(x, axis, [(i, i ^ k) for i in range(size)])


def after(x, *others):
    return lax.optimization_barrier((x, *others))[0]


def swap_two(x, n_enc, k, n_col, j):
    moves = [
        (e * n_col + c, (e ^ k) * n_col + (c ^ j)) for e in range(n_enc) for c in range(n_col)
    ]
    return lax.ppermute(x, ("enc", "col"), moves)


def kernel_call(body, out_shape, cost=(0, 0, 0), **kw):
    return pl.pallas_call(
        body,
        out_shape=out_shape,
        compiler_params=pltpu.CompilerParams(vmem_limit_bytes=VMEM_LIMIT),
        cost_estimate=pl.CostEstimate(flops=cost[0], bytes_accessed=cost[1], transcendentals=cost[2]),
        **kw,
    )


def rope_tables(positions):
    half = HEAD_DIM // 2
    part_side = HEAD_DIM // 6
    part_time = half - 2 * part_side
    freq_time = 1.0 / 10000.0 ** (jnp.arange(part_time, dtype=jnp.float32) * 2.0 / (2 * part_time))
    freq_side = 1.0 / 10000.0 ** (jnp.arange(part_side, dtype=jnp.float32) * 2.0 / (2 * part_side))
    freq = jnp.repeat(jnp.concatenate([freq_time, freq_side, freq_side]), 2)
    pair = np.arange(HEAD_DIM) // 2
    coords = positions.astype(jnp.float32)
    coord = jnp.where(
        pair < part_time,
        coords[:, 0:1],
        jnp.where(pair < part_time + part_side, coords[:, 1:2], coords[:, 2:3]),
    )
    angles = coord * freq
    sign = np.where(np.arange(HEAD_DIM) % 2 == 0, -1.0, 1.0).astype(np.float32)
    return jnp.cos(angles), jnp.sin(angles) * sign


def columns_of(axis, k, width):
    start = (lax.axis_index(axis) ^ k) * width
    return pl.ds(pl.multiple_of(start, HEAD_DIM), width)


def join_rows(pieces, others, axis):
    rows, width = pieces[0].shape
    parts = len(pieces)
    n = parts + len(others)

    def body(*refs):
        for k in range(parts):
            start = (lax.axis_index(axis) ^ k) * rows
            here = pl.ds(pl.multiple_of(start, math.gcd(rows, 32)), rows)
            refs[n][here, :] = refs[k][...]
            refs[n + 1][0, here, :] = refs[k][...]
        for i, ref in enumerate(refs[parts:n]):
            refs[n + 1][i + 1] = ref[...]

    return kernel_call(
        body,
        [
            jax.ShapeDtypeStruct((rows * parts, width), pieces[0].dtype),
            jax.ShapeDtypeStruct((1 + len(others), rows * parts, width), pieces[0].dtype),
        ],
    )(*pieces, *others)


def join_columns(pieces, axis):
    rows, piece = pieces[0].shape
    parts = len(pieces)

    def body(*refs):
        copies = [
            pltpu.make_async_copy(
                refs[k], refs[parts].at[:, columns_of(axis, k, piece)], refs[parts + 1].at[k]
            )
            for k in range(parts)
        ]
        for copy in copies:
            copy.start()
        for copy in copies:
            copy.wait()

    return kernel_call(
        body,
        jax.ShapeDtypeStruct((rows, piece * parts), pieces[0].dtype),
        in_specs=[pl.BlockSpec(memory_space=pl.ANY)] * parts,
        out_specs=pl.BlockSpec(memory_space=pl.ANY),
        scratch_shapes=[pltpu.SemaphoreType.DMA((parts,))],
    )(*pieces)


def split_sum(x, y, parts):
    kinds, count, width = x.shape
    part = count // parts

    def body(x_ref, y_ref, *outs):
        for k in range(parts):
            here = slice(k * part, (k + 1) * part)
            outs[k][...] = x_ref[:, here] + y_ref[:, here]

    return kernel_call(body, [jax.ShapeDtypeStruct((kinds, part, width), x.dtype)] * parts)(x, y)


def square_sums(queries, keys):
    rows, width = queries.shape

    def body(q_ref, k_ref, out_ref):
        for i, ref in enumerate((q_ref, k_ref)):
            wide = ref[...].astype(jnp.float32)
            out_ref[:, i : i + 1] = jnp.sum(wide * wide, axis=1, keepdims=True)

    return kernel_call(
        body, jax.ShapeDtypeStruct((rows, 2), jnp.float32), (4 * rows * width, 4 * rows * width, 0)
    )(queries, keys)


def context_factor(wide):
    return lax.rsqrt(jnp.mean(wide * wide, axis=1, keepdims=True) + eps)


def context_shards(keys, values, gain, width, axis, parts):
    rows = keys.shape[0]

    def body(k_ref, v_ref, gain_ref, *outs):
        wide = k_ref[...].astype(jnp.float32)
        recip = context_factor(wide)
        for k in range(parts):
            cols = columns_of(axis, k, width)
            part = k_ref[:, cols].astype(jnp.float32) * recip * gain_ref[:, cols]
            outs[k][0] = part.astype(jnp.bfloat16)
            outs[k][1] = v_ref[:, cols]

    return kernel_call(body, [jax.ShapeDtypeStruct((2, rows, width), jnp.bfloat16)] * parts)(
        keys, values, gain[None, :]
    )


def context_gradients(keys, gain, pieces, axis):
    rows, full = keys.shape
    parts = len(pieces)
    width = full // parts
    flat = [x for piece in pieces for x in piece]

    def body(k_ref, gain_ref, *refs):
        grad_ref, values_ref, scaled = refs[len(flat) :]
        at = 0
        for k, piece in enumerate(pieces):
            total = refs[at][...]
            for i in range(1, len(piece)):
                total = total + refs[at + i][...]
            at += len(piece)
            cols = columns_of(axis, k, width)
            scaled[:, cols] = gain_ref[:, cols] * total[0]
            values_ref[:, cols] = total[1]
        wide = k_ref[...].astype(jnp.float32)
        recip = context_factor(wide)
        inner = jnp.mean(wide * scaled[...], axis=1, keepdims=True)
        grad_ref[...] = recip * scaled[...] - wide * (recip * recip * recip) * inner

    return kernel_call(
        body,
        [jax.ShapeDtypeStruct((rows, full), jnp.float32)] * 2,
        scratch_shapes=[pltpu.VMEM((rows, full), jnp.float32)],
    )(keys, gain[None, :], *flat)


def norm_factor(total_refs, which, full_width):
    total = total_refs[0][:, which : which + 1]
    for ref in total_refs[1:]:
        total = total + ref[:, which : which + 1]
    return lax.rsqrt(total / full_width + eps)


def normed_turned(x, which, totals, gain, cosine, sine, full_width, axis, parts, relative):
    rows, width = x.shape
    piece = width // parts
    n_totals = len(totals)

    def body(*refs):
        x_ref, gain_ref, cos_ref, sin_ref = refs[n_totals : n_totals + 4]
        outs = refs[n_totals + 4 :]
        recip = norm_factor(refs[:n_totals], which, full_width)
        cos = cos_ref[...]
        sin = sin_ref[...]
        even = lax.broadcasted_iota(jnp.int32, cos.shape, 1) % 2 == 0
        for k in range(parts):
            for h in range(piece // HEAD_DIM):
                start = k * piece + h * HEAD_DIM
                if parts > 1 and relative:
                    start = pl.multiple_of(
                        (lax.axis_index(axis) ^ k) * piece + h * HEAD_DIM, HEAD_DIM
                    )
                cols = pl.ds(start, HEAD_DIM)
                here = slice(h * HEAD_DIM, (h + 1) * HEAD_DIM)
                normed = x_ref[:, cols].astype(jnp.float32) * recip * gain_ref[:, cols]
                other = jnp.where(
                    even, pltpu.roll(normed, HEAD_DIM - 1, 1), pltpu.roll(normed, 1, 1)
                )
                turned = (normed * cos + other * sin).astype(jnp.bfloat16)
                if relative:
                    outs[k][:, here] = turned
                else:
                    outs[0][k, :, here] = turned

    shapes = [(rows, piece)] * parts if relative else [(parts, rows, piece)]
    return kernel_call(body, [jax.ShapeDtypeStruct(sh, jnp.bfloat16) for sh in shapes])(
        *totals, x, gain[None, :], cosine, sine
    )


def attention(query, keys, values):
    rows, width = query.shape
    factor = HEAD_DIM ** (-0.5) * LOG2E
    heads = [slice(h, h + HEAD_DIM) for h in range(0, width, HEAD_DIM)]
    pairs = [x if isinstance(x, tuple) else (x, None) for x in (*keys, *values)]
    arrays = []
    for x, _ in pairs:
        if not any(x is y for y in arrays):
            arrays.append(x)
    places = [(next(i for i, y in enumerate(arrays) if y is x), at) for x, at in pairs]

    def body(q_ref, *refs):
        def part(place, cols):
            i, at = place
            return refs[i][:, cols] if at is None else refs[i][at, :, cols]

        def scores(cols):
            q = q_ref[:, cols]
            return [
                lax.dot_general(q, part(place, cols), NT, preferred_element_type=jnp.float32)
                for place in places[: len(keys)]
            ]

        following = scores(heads[0])
        for j, cols in enumerate(heads):
            current = following
            if j + 1 < len(heads):
                following = scores(heads[j + 1])
            peak = functools.reduce(
                jnp.maximum, [jnp.max(s, axis=1, keepdims=True) for s in current]
            )
            weight_sum = 0.0
            mixed = 0.0
            for s, place in zip(current, places[len(keys) :]):
                weights = jnp.exp2((s - peak) * factor)
                weight_sum = weight_sum + jnp.sum(weights, axis=1, keepdims=True)
                mixed = mixed + jnp.dot(
                    weights.astype(jnp.bfloat16),
                    part(place, cols),
                    preferred_element_type=jnp.float32,
                )
            refs[-1][:, cols] = (mixed / weight_sum).astype(jnp.bfloat16)

    return kernel_call(body, jax.ShapeDtypeStruct((rows, width), jnp.bfloat16))(query, *arrays)


def image_attention(queries, totals, gain, full_width, context, cotangent):
    rows, width = queries.shape
    n_totals = len(totals)
    count = context.shape[1]
    heads = width // HEAD_DIM
    half = count // 2
    scale = HEAD_DIM ** (-0.5)

    def body(*refs):
        q_ref, gain_ref, c_ref, g_ref, out_ref, keep_ref, send_ref = refs[n_totals:]
        recip = norm_factor(refs[:n_totals], 0, full_width)
        for h in range(heads):
            cols = slice(h * HEAD_DIM, (h + 1) * HEAD_DIM)
            q = (q_ref[:, cols].astype(jnp.float32) * recip * gain_ref[:, cols]).astype(jnp.bfloat16)
            g = g_ref[:, cols]
            k = c_ref[0, :, cols]
            v = c_ref[1, :, cols]
            scores = lax.dot_general(k, q, NT, preferred_element_type=jnp.float32) * scale
            weights = jnp.exp(scores - jnp.max(scores, axis=0, keepdims=True))
            probs = weights / jnp.sum(weights, axis=0, keepdims=True)
            low = probs.astype(jnp.bfloat16)
            out_ref[:, cols] = lax.dot_general(
                low, v, TN, preferred_element_type=jnp.float32
            ).astype(jnp.bfloat16)
            grad_v = jnp.dot(low, g, preferred_element_type=jnp.float32)
            grad_p = lax.dot_general(v, g, NT, preferred_element_type=jnp.float32)
            inner = jnp.sum(probs * grad_p, axis=0, keepdims=True)
            grad_s = (probs * (grad_p - inner)).astype(jnp.bfloat16)
            grad_k = jnp.dot(grad_s, q, preferred_element_type=jnp.float32) * scale
            for i, grad in enumerate((grad_k, grad_v)):
                keep_ref[i, :, cols] = grad[:half]
                send_ref[i, :, cols] = grad[half:]

    return kernel_call(
        body,
        [
            jax.ShapeDtypeStruct((rows, width), jnp.bfloat16),
            jax.ShapeDtypeStruct((2, half, width), jnp.float32),
            jax.ShapeDtypeStruct((2, half, width), jnp.float32),
        ],
        (10 * rows * count * width, 80 * rows * width, rows * count * heads),
    )(*totals, queries, gain[None, :], context, cotangent)


def per_device(
    sizes,
    queries,
    self_keys,
    self_values,
    positions,
    query_gain,
    key_gain,
    context_keys,
    context_values,
    context_gain,
    image_cotangent,
):
    n_enc, n_row, n_col = sizes
    rows, width = queries.shape
    heads = width // HEAD_DIM
    full_width = width * n_enc
    row_bits = [1 << i for i in reversed(range(n_row.bit_length() - 1))]
    parts = n_col if heads % n_col == 0 and len(row_bits) == 2 else 1

    def relay(x):
        if parts == 1:
            return x
        return lax.all_to_all(x, "col", split_axis=0, concat_axis=0, tiled=True)

    value_split = jnp.swapaxes(self_values.reshape(rows, parts, width // parts), 0, 1)
    values_here = relay(value_split)

    own_count = context_keys.shape[0]
    context = context_shards(after(context_keys, value_split), context_values, context_gain, width, "enc", n_enc)
    context = [swap(x, "enc", n_enc, k) if k else x for k, x in enumerate(context)]
    sums = square_sums(after(queries, context[0]), self_keys)
    totals = [sums]
    bit = 1
    while bit < n_enc:
        if len(totals) > 1:
            totals = [totals[0] + totals[1]]
        totals = [totals[0], swap(totals[0], "enc", n_enc, bit)]
        bit *= 2
    cosine, sine = rope_tables(after(positions, sums))
    key_pieces = normed_turned(
        self_keys, 1, totals, key_gain, cosine, sine, full_width, "col", parts, True
    )
    context = jnp.concatenate(context, axis=1)
    bit = n_row // 2
    while bit:
        other = after(swap(context, "row", n_row, bit), key_pieces[0])
        context = jnp.concatenate([context, other], axis=1)
        bit //= 2
    key_pieces = [swap(x, "col", n_col, k) if k else x for k, x in enumerate(key_pieces)]

    values_here = after(values_here, key_pieces[0]).reshape(parts * rows, width // parts)
    image_out, grad, sent = image_attention(
        queries, totals, query_gain, full_width, after(context, values_here), image_cotangent
    )
    all_values = [values_here]
    if parts > 1:
        all_values += [swap(values_here, "row", n_row, row_bits[0])]
    key_pieces = [key_pieces[0], *(after(x, grad) for x in key_pieces[1:])]
    keys_here, bundle = join_rows(key_pieces, all_values, "col")
    query_here = normed_turned(
        after(queries, keys_here), 0, totals, query_gain, cosine, sine, full_width, "col", parts, True
    )
    got = keys_here
    if parts > 1:
        keys_there = swap(keys_here, "row", n_row, row_bits[0])
        query_here = [swap(x, "col", n_col, k) if k else x for k, x in enumerate(query_here)]
        got = swap(bundle, "row", n_row, row_bits[1])
        all_values += [(got, 1), (got, 2)]
        all_keys = [keys_here, keys_there, (got, 0)]
    else:
        all_keys = [lax.all_gather(keys_here, ("row", "col"), axis=0, tiled=True)]
        all_values = [lax.all_gather(values_here, ("row", "col"), axis=0, tiled=True)]

    for i in range(len(row_bits)):
        got = swap(after(sent, got), "row", n_row, 1 << i)
        if i + 1 < len(row_bits):
            grad, sent = split_sum(grad, got, 2)
        else:
            grad = split_sum(grad, got, 1)[0]
    if parts > 1:
        keys_there = after(keys_there, grad, *query_here)
        all_keys += [swap(keys_there, "row", n_row, row_bits[1])]

    mixed = [None] * parts
    col_bits = [1 << i for i in reversed(range(n_col.bit_length() - 1))]
    for bit in col_bits[:-1]:
        got = swap(grad, "col", n_col, bit)
        if bit > 2:
            grad = split_sum(grad, got, 1)[0]
    for i, k in enumerate(reversed(range(parts))):
        piece = attention(query_here[k], all_keys, all_values)
        mixed[k] = swap(piece, "col", n_col, k) if k else piece
        if i == min(1, parts - 1):
            got = after(got, piece)
    sent = split_sum(grad, got, n_enc)
    grad = []
    for k, x in enumerate(sent):
        grad.append([swap(x, "enc", n_enc, k) if k else x, swap_two(x, n_enc, k, n_col, col_bits[-1])])
    grad[0][0] = after(grad[0][0], mixed[0])
    grad_keys_in, grad_values_in = context_gradients(context_keys, context_gain, grad, "enc")
    self_out = join_columns(mixed, "col") if parts > 1 else mixed[0]

    return (self_out, image_out, grad_keys_in, grad_values_in)


def solution(mesh):
    sizes = tuple(mesh.shape[a] for a in ("enc", "row", "col"))
    return jax.shard_map(
        functools.partial(per_device, sizes),
        mesh=mesh,
        in_specs=(
            P(("row", "col"), "enc"),
            P(("row", "col"), "enc"),
            P(("row", "col"), "enc"),
            P(("row", "col"), None),
            P("enc"),
            P("enc"),
            P(("enc", "row"), None),
            P(("enc", "row"), None),
            P(),
            P(("row", "col"), "enc"),
        ),
        out_specs=(
            P(("row", "col"), "enc"),
            P(("row", "col"), "enc"),
            P(("enc", "row"), None),
            P(("enc", "row"), None),
        ),
        check_vma=False,
    )
```

```python
import functools
import math

import jax
import jax.numpy as jnp
import numpy as np
from jax import lax
from jax.experimental import pallas as pl
from jax.experimental.pallas import tpu as pltpu
from jax.sharding import PartitionSpec as P

HEAD_DIM = 128
eps = 1e-06
LOG2E = 1.4426950408889634
NT = (((1,), (1,)), ((), ()))
TN = (((0,), (0,)), ((), ()))
VMEM_LIMIT = 20 * 1024 * 1024


def swap(x, axis, size, k):
    return lax.ppermute(x, axis, [(i, i ^ k) for i in range(size)])


def after(x, *others):
    return lax.optimization_barrier((x, *others))[0]


def swap_two(x, n_enc, k, n_col, j):
    moves = [
        (e * n_col + c, (e ^ k) * n_col + (c ^ j)) for e in range(n_enc) for c in range(n_col)
    ]
    return lax.ppermute(x, ("enc", "col"), moves)


def kernel_call(body, out_shape, cost=(0, 0, 0), vmem=VMEM_LIMIT, **kw):
    return pl.pallas_call(
        body,
        out_shape=out_shape,
        compiler_params=pltpu.CompilerParams(vmem_limit_bytes=vmem),
        cost_estimate=pl.CostEstimate(flops=cost[0], bytes_accessed=cost[1], transcendentals=cost[2]),
        **kw,
    )


def rope_tables(positions):
    half = HEAD_DIM // 2
    part_side = HEAD_DIM // 6
    part_time = half - 2 * part_side
    freq_time = 1.0 / 10000.0 ** (jnp.arange(part_time, dtype=jnp.float32) * 2.0 / (2 * part_time))
    freq_side = 1.0 / 10000.0 ** (jnp.arange(part_side, dtype=jnp.float32) * 2.0 / (2 * part_side))
    freq = jnp.repeat(jnp.concatenate([freq_time, freq_side, freq_side]), 2)
    pair = np.arange(HEAD_DIM) // 2
    coords = positions.astype(jnp.float32)
    coord = jnp.where(
        pair < part_time,
        coords[:, 0:1],
        jnp.where(pair < part_time + part_side, coords[:, 1:2], coords[:, 2:3]),
    )
    angles = coord * freq
    sign = np.where(np.arange(HEAD_DIM) % 2 == 0, -1.0, 1.0).astype(np.float32)
    return jnp.cos(angles), jnp.sin(angles) * sign


def columns_of(axis, k, width):
    start = (lax.axis_index(axis) ^ k) * width
    return pl.ds(pl.multiple_of(start, HEAD_DIM), width)


def split_columns(x, parts):
    rows, width = x.shape
    piece = width // parts

    def body(x_ref, out_ref, sems):
        copies = [
            pltpu.make_async_copy(x_ref.at[:, pl.ds(z * piece, piece)], out_ref.at[z], sems.at[z])
            for z in range(parts)
        ]
        for copy in copies:
            copy.start()
        for copy in copies:
            copy.wait()

    return kernel_call(
        body,
        jax.ShapeDtypeStruct((parts, rows, piece), x.dtype),
        in_specs=[pl.BlockSpec(memory_space=pltpu.VMEM)],
        out_specs=pl.BlockSpec(memory_space=pl.ANY),
        scratch_shapes=[pltpu.SemaphoreType.DMA((parts,))],
    )(x)


def join_rows(pieces, others, axis):
    rows, width = pieces[0].shape
    parts = len(pieces)
    n = parts + len(others)

    def body(*refs):
        for k in range(parts):
            start = (lax.axis_index(axis) ^ k) * rows
            here = pl.ds(pl.multiple_of(start, math.gcd(rows, 32)), rows)
            refs[n][here, :] = refs[k][...]
            refs[n + 1][0, here, :] = refs[k][...]
        for i, ref in enumerate(refs[parts:n]):
            refs[n + 1][i + 1] = ref[...]

    return kernel_call(
        body,
        [
            jax.ShapeDtypeStruct((rows * parts, width), pieces[0].dtype),
            jax.ShapeDtypeStruct((1 + len(others), rows * parts, width), pieces[0].dtype),
        ],
    )(*pieces, *others)


def join_columns(pieces, axis):
    rows, piece = pieces[0].shape
    parts = len(pieces)

    def body(*refs):
        copies = [
            pltpu.make_async_copy(
                refs[k], refs[parts].at[:, columns_of(axis, k, piece)], refs[parts + 1].at[k]
            )
            for k in range(parts)
        ]
        for copy in copies:
            copy.start()
        for copy in copies:
            copy.wait()

    return kernel_call(
        body,
        jax.ShapeDtypeStruct((rows, piece * parts), pieces[0].dtype),
        in_specs=[pl.BlockSpec(memory_space=pl.ANY)] * parts,
        out_specs=pl.BlockSpec(memory_space=pl.ANY),
        scratch_shapes=[pltpu.SemaphoreType.DMA((parts,))],
    )(*pieces)


def split_sum(x, y, parts):
    kinds, count, width = x.shape
    part = count // parts

    def body(x_ref, y_ref, *outs):
        for k in range(parts):
            here = slice(k * part, (k + 1) * part)
            outs[k][...] = x_ref[:, here] + y_ref[:, here]

    return kernel_call(body, [jax.ShapeDtypeStruct((kinds, part, width), x.dtype)] * parts)(x, y)


def square_sums(queries, keys):
    rows, width = queries.shape

    def body(q_ref, k_ref, out_ref):
        for i, ref in enumerate((q_ref, k_ref)):
            wide = ref[...].astype(jnp.float32)
            out_ref[:, i : i + 1] = jnp.sum(wide * wide, axis=1, keepdims=True)

    return kernel_call(
        body, jax.ShapeDtypeStruct((rows, 2), jnp.float32), (4 * rows * width, 4 * rows * width, 0)
    )(queries, keys)


def context_factor(wide):
    return lax.rsqrt(jnp.mean(wide * wide, axis=1, keepdims=True) + eps)


def context_shards(keys, values, gain, width, axis, parts):
    rows = keys.shape[0]

    def body(k_ref, v_ref, gain_ref, *outs):
        wide = k_ref[...].astype(jnp.float32)
        recip = context_factor(wide)
        for k in range(parts):
            cols = columns_of(axis, k, width)
            part = k_ref[:, cols].astype(jnp.float32) * recip * gain_ref[:, cols]
            outs[k][0] = part.astype(jnp.bfloat16)
            outs[k][1] = v_ref[:, cols]

    return kernel_call(body, [jax.ShapeDtypeStruct((2, rows, width), jnp.bfloat16)] * parts)(
        keys, values, gain[None, :]
    )


def context_gradients(keys, gain, pieces, axis):
    rows, full = keys.shape
    parts = len(pieces)
    width = full // parts
    flat = [x for piece in pieces for x in piece]

    def body(k_ref, gain_ref, *refs):
        grad_ref, values_ref, scaled = refs[len(flat) :]
        at = 0
        for k, piece in enumerate(pieces):
            total = refs[at][...]
            for i in range(1, len(piece)):
                total = total + refs[at + i][...]
            at += len(piece)
            cols = columns_of(axis, k, width)
            scaled[:, cols] = gain_ref[:, cols] * total[0]
            values_ref[:, cols] = total[1]
        wide = k_ref[...].astype(jnp.float32)
        recip = context_factor(wide)
        inner = jnp.mean(wide * scaled[...], axis=1, keepdims=True)
        grad_ref[...] = recip * scaled[...] - wide * (recip * recip * recip) * inner

    return kernel_call(
        body,
        [jax.ShapeDtypeStruct((rows, full), jnp.float32)] * 2,
        scratch_shapes=[pltpu.VMEM((rows, full), jnp.float32)],
    )(keys, gain[None, :], *flat)


def norm_factor(total_refs, which, full_width):
    total = total_refs[0][:, which : which + 1]
    for ref in total_refs[1:]:
        total = total + ref[:, which : which + 1]
    return lax.rsqrt(total / full_width + eps)


def normed_turned(x, which, totals, gain, cosine, sine, full_width, axis, parts, relative):
    rows, width = x.shape
    piece = width // parts
    n_totals = len(totals)

    def body(*refs):
        x_ref, gain_ref, cos_ref, sin_ref = refs[n_totals : n_totals + 4]
        outs = refs[n_totals + 4 :]
        recip = norm_factor(refs[:n_totals], which, full_width)
        cos = cos_ref[...]
        sin = sin_ref[...]
        even = lax.broadcasted_iota(jnp.int32, cos.shape, 1) % 2 == 0
        for k in range(parts):
            for h in range(piece // HEAD_DIM):
                start = k * piece + h * HEAD_DIM
                if parts > 1 and relative:
                    start = pl.multiple_of(
                        (lax.axis_index(axis) ^ k) * piece + h * HEAD_DIM, HEAD_DIM
                    )
                cols = pl.ds(start, HEAD_DIM)
                here = slice(h * HEAD_DIM, (h + 1) * HEAD_DIM)
                normed = x_ref[:, cols].astype(jnp.float32) * recip * gain_ref[:, cols]
                other = jnp.where(
                    even, pltpu.roll(normed, HEAD_DIM - 1, 1), pltpu.roll(normed, 1, 1)
                )
                turned = (normed * cos + other * sin).astype(jnp.bfloat16)
                if relative:
                    outs[k][:, here] = turned
                else:
                    outs[0][k, :, here] = turned

    shapes = [(rows, piece)] * parts if relative else [(parts, rows, piece)]
    return kernel_call(body, [jax.ShapeDtypeStruct(sh, jnp.bfloat16) for sh in shapes])(
        *totals, x, gain[None, :], cosine, sine
    )


def attention(query, keys, values):
    rows, width = query.shape
    factor = HEAD_DIM ** (-0.5) * LOG2E
    heads = [slice(h, h + HEAD_DIM) for h in range(0, width, HEAD_DIM)]
    pairs = [x if isinstance(x, tuple) else (x, None) for x in (*keys, *values)]
    arrays = []
    for x, _ in pairs:
        if not any(x is y for y in arrays):
            arrays.append(x)
    places = [(next(i for i, y in enumerate(arrays) if y is x), at) for x, at in pairs]

    def body(q_ref, *refs):
        def part(place, cols):
            i, at = place
            return refs[i][:, cols] if at is None else refs[i][at, :, cols]

        def scores(cols):
            q = q_ref[:, cols]
            return [
                lax.dot_general(q, part(place, cols), NT, preferred_element_type=jnp.float32)
                for place in places[: len(keys)]
            ]

        following = scores(heads[0])
        for j, cols in enumerate(heads):
            current = following
            if j + 1 < len(heads):
                following = scores(heads[j + 1])
            peak = functools.reduce(
                jnp.maximum, [jnp.max(s, axis=1, keepdims=True) for s in current]
            )
            weight_sum = 0.0
            mixed = 0.0
            for s, place in zip(current, places[len(keys) :]):
                weights = jnp.exp2((s - peak) * factor)
                weight_sum = weight_sum + jnp.sum(weights, axis=1, keepdims=True)
                mixed = mixed + jnp.dot(
                    weights.astype(jnp.bfloat16),
                    part(place, cols),
                    preferred_element_type=jnp.float32,
                )
            refs[-1][:, cols] = (mixed / weight_sum).astype(jnp.bfloat16)

    return kernel_call(body, jax.ShapeDtypeStruct((rows, width), jnp.bfloat16))(query, *arrays)


def image_attention(queries, totals, gain, full_width, context, cotangent):
    rows, width = queries.shape
    n_totals = len(totals)
    count = context.shape[1]
    half = count // 2
    scale = HEAD_DIM ** (-0.5)

    def body(*refs):
        q_ref, gain_ref, c_ref, g_ref, out_ref, keep_ref, send_ref = refs[n_totals:]
        recip = norm_factor(refs[:n_totals], 0, full_width)
        sides = [slice(h, h + HEAD_DIM) for h in range(0, width, HEAD_DIM)]
        heads = []
        for cols in sides:
            q = (q_ref[:, cols].astype(jnp.float32) * recip * gain_ref[:, cols]).astype(jnp.bfloat16)
            scores = scale * lax.dot_general(
                c_ref[0, :, cols], q, NT, preferred_element_type=jnp.float32
            )
            grad_p = lax.dot_general(
                c_ref[1, :, cols], g_ref[:, cols], NT, preferred_element_type=jnp.float32
            )
            heads.append((q, scores, grad_p))
        rounded = []
        for q, scores, grad_p in heads:
            weights = jnp.exp(scores - jnp.max(scores, axis=0, keepdims=True))
            probs = weights / jnp.sum(weights, axis=0, keepdims=True)
            inner = jnp.sum(probs * grad_p, axis=0, keepdims=True)
            grad_s = probs * (grad_p - inner)
            rounded.append((q, probs.astype(jnp.bfloat16), grad_s.astype(jnp.bfloat16)))
        for cols, (q, low, grad_s) in zip(sides, rounded):
            out_ref[:, cols] = lax.dot_general(
                low, c_ref[1, :, cols], TN, preferred_element_type=jnp.float32
            ).astype(jnp.bfloat16)
            grad_v = jnp.dot(low, g_ref[:, cols], preferred_element_type=jnp.float32)
            grad_k = jnp.dot(grad_s, q, preferred_element_type=jnp.float32) * scale
            for i, grad in enumerate((grad_k, grad_v)):
                keep_ref[i, :, cols] = grad[:half]
                send_ref[i, :, cols] = grad[half:]

    return kernel_call(
        body,
        [
            jax.ShapeDtypeStruct((rows, width), jnp.bfloat16),
            jax.ShapeDtypeStruct((2, half, width), jnp.float32),
            jax.ShapeDtypeStruct((2, half, width), jnp.float32),
        ],
        (1000, 1000, 0),
    )(*totals, queries, gain[None, :], context, cotangent)


def per_device(
    sizes,
    queries,
    self_keys,
    self_values,
    positions,
    query_gain,
    key_gain,
    context_keys,
    context_values,
    context_gain,
    image_cotangent,
):
    n_enc, n_row, n_col = sizes
    rows, width = queries.shape
    heads = width // HEAD_DIM
    full_width = width * n_enc
    row_bits = [1 << i for i in reversed(range(n_row.bit_length() - 1))]
    parts = n_col if heads % n_col == 0 and len(row_bits) == 2 else 1

    def relay(x):
        if parts == 1:
            return x
        return lax.all_to_all(x, "col", split_axis=0, concat_axis=0, tiled=True)

    value_split = split_columns(self_values, parts)
    values_here = relay(value_split)

    own_count = context_keys.shape[0]
    context = context_shards(after(context_keys, value_split), context_values, context_gain, width, "enc", n_enc)
    context = [swap(x, "enc", n_enc, k) if k else x for k, x in enumerate(context)]
    sums = square_sums(after(queries, context[0]), self_keys)
    totals = [sums]
    bit = 1
    while bit < n_enc:
        if len(totals) > 1:
            totals = [totals[0] + totals[1]]
        totals = [totals[0], swap(totals[0], "enc", n_enc, bit)]
        bit *= 2
    cosine, sine = rope_tables(after(positions, sums))
    key_pieces = normed_turned(
        self_keys, 1, totals, key_gain, cosine, sine, full_width, "col", parts, True
    )
    context = jnp.concatenate(context, axis=1)
    bit = n_row // 2
    while bit:
        other = after(swap(context, "row", n_row, bit), key_pieces[0])
        context = jnp.concatenate([context, other], axis=1)
        bit //= 2
    key_pieces = [swap(x, "col", n_col, k) if k else x for k, x in enumerate(key_pieces)]

    image_out, grad, sent = image_attention(
        queries, totals, query_gain, full_width, context, image_cotangent
    )
    values_here = after(values_here, context).reshape(parts * rows, width // parts)

    all_values = [values_here]
    if parts > 1:
        all_values += [swap(values_here, "row", n_row, row_bits[0])]
    query_here = normed_turned(
        after(queries, grad), 0, totals, query_gain, cosine, sine, full_width, "col", parts, True
    )
    key_pieces = [key_pieces[0], *(after(x, values_here, *query_here) for x in key_pieces[1:])]
    keys_here, bundle = join_rows(key_pieces, all_values, "col")
    got = keys_here
    if parts > 1:
        keys_there = swap(keys_here, "row", n_row, row_bits[0])
        query_here = [swap(x, "col", n_col, k) if k else x for k, x in enumerate(query_here)]
        across = swap(bundle, "row", n_row, row_bits[1])
        all_values += [(across, 1), (across, 2)]
        all_keys = [keys_here, keys_there, (across, 0)]
        got = across
    else:
        all_keys = [lax.all_gather(keys_here, ("row", "col"), axis=0, tiled=True)]
        all_values = [lax.all_gather(values_here, ("row", "col"), axis=0, tiled=True)]

    for i in range(len(row_bits)):
        if i + 1 < len(row_bits):
            grad, sent = split_sum(grad, after(swap(sent, "row", n_row, 1 << i), keys_here), 2)
        else:
            grad = split_sum(grad, swap(after(sent, got), "row", n_row, 1 << i), 1)[0]
    if parts > 1:
        keys_there = after(keys_there, grad, across, *query_here)
        all_keys += [swap(keys_there, "row", n_row, row_bits[1])]

    mixed = [None] * parts
    col_bits = [1 << i for i in reversed(range(n_col.bit_length() - 1))]
    for bit in col_bits[:-2]:
        grad = split_sum(grad, swap(grad, "col", n_col, bit), 1)[0]
    steps = col_bits[-2:]
    got = swap(grad, "col", n_col, steps[0])
    for i, k in enumerate(reversed(range(parts))):
        piece = attention(query_here[k], all_keys, all_values)
        mixed[k] = swap(piece, "col", n_col, k) if k else piece
        if i == 0:
            got = after(got, piece)
    if len(steps) > 1:
        grad = split_sum(grad, got, 1)[0]
        got = after(swap(grad, "col", n_col, steps[1]), mixed[0])
    grad = split_sum(grad, got, n_enc)
    grad = [[swap(x, "enc", n_enc, k) if k else x] for k, x in enumerate(grad)]
    grad_keys_in, grad_values_in = context_gradients(context_keys, context_gain, grad, "enc")
    self_out = join_columns(mixed, "col") if parts > 1 else mixed[0]

    return (self_out, image_out, grad_keys_in, grad_values_in)


def solution(mesh):
    sizes = tuple(mesh.shape[a] for a in ("enc", "row", "col"))
    return jax.shard_map(
        functools.partial(per_device, sizes),
        mesh=mesh,
        in_specs=(
            P(("row", "col"), "enc"),
            P(("row", "col"), "enc"),
            P(("row", "col"), "enc"),
            P(("row", "col"), None),
            P("enc"),
            P("enc"),
            P(("enc", "row"), None),
            P(("enc", "row"), None),
            P(),
            P(("row", "col"), "enc"),
        ),
        out_specs=(
            P(("row", "col"), "enc"),
            P(("row", "col"), "enc"),
            P(("enc", "row"), None),
            P(("enc", "row"), None),
        ),
        check_vma=False,
    )
```

```python
import functools
import math

import jax
import jax.numpy as jnp
import numpy as np
from jax import lax
from jax.experimental import pallas as pl
from jax.experimental.pallas import tpu as pltpu
from jax.sharding import PartitionSpec as P

HEAD_DIM = 128
eps = 1e-06
LOG2E = 1.4426950408889634
NT = (((1,), (1,)), ((), ()))
TN = (((0,), (0,)), ((), ()))
VMEM_LIMIT = 20 * 1024 * 1024


def swap(x, axis, size, k):
    return lax.ppermute(x, axis, [(i, i ^ k) for i in range(size)])


def after(x, *others):
    return lax.optimization_barrier((x, *others))[0]


def swap_two(x, n_enc, k, n_col, j):
    moves = [
        (e * n_col + c, (e ^ k) * n_col + (c ^ j)) for e in range(n_enc) for c in range(n_col)
    ]
    return lax.ppermute(x, ("enc", "col"), moves)


def kernel_call(body, out_shape, cost=(0, 0, 0), vmem=VMEM_LIMIT, **kw):
    return pl.pallas_call(
        body,
        out_shape=out_shape,
        compiler_params=pltpu.CompilerParams(vmem_limit_bytes=vmem),
        cost_estimate=pl.CostEstimate(flops=cost[0], bytes_accessed=cost[1], transcendentals=cost[2]),
        **kw,
    )


def rope_tables(positions):
    half = HEAD_DIM // 2
    part_side = HEAD_DIM // 6
    part_time = half - 2 * part_side
    freq_time = 1.0 / 10000.0 ** (jnp.arange(part_time, dtype=jnp.float32) * 2.0 / (2 * part_time))
    freq_side = 1.0 / 10000.0 ** (jnp.arange(part_side, dtype=jnp.float32) * 2.0 / (2 * part_side))
    freq = jnp.repeat(jnp.concatenate([freq_time, freq_side, freq_side]), 2)
    pair = np.arange(HEAD_DIM) // 2
    coords = positions.astype(jnp.float32)
    coord = jnp.where(
        pair < part_time,
        coords[:, 0:1],
        jnp.where(pair < part_time + part_side, coords[:, 1:2], coords[:, 2:3]),
    )
    angles = coord * freq
    sign = np.where(np.arange(HEAD_DIM) % 2 == 0, -1.0, 1.0).astype(np.float32)
    return jnp.cos(angles), jnp.sin(angles) * sign


def columns_of(axis, k, width):
    start = (lax.axis_index(axis) ^ k) * width
    return pl.ds(pl.multiple_of(start, HEAD_DIM), width)


def split_columns(x, parts):
    rows, width = x.shape
    piece = width // parts

    def body(x_ref, out_ref):
        for z in range(parts):
            out_ref[z] = x_ref[:, z * piece : (z + 1) * piece]

    return kernel_call(body, jax.ShapeDtypeStruct((parts, rows, piece), x.dtype))(x)


def join_rows(pieces, others, axis):
    rows, width = pieces[0].shape
    parts = len(pieces)
    n = parts + len(others)

    def body(*refs):
        for k in range(parts):
            start = (lax.axis_index(axis) ^ k) * rows
            here = pl.ds(pl.multiple_of(start, math.gcd(rows, 32)), rows)
            refs[n][here, :] = refs[k][...]
            refs[n + 1][0, here, :] = refs[k][...]
        for i, ref in enumerate(refs[parts:n]):
            refs[n + 1][i + 1] = ref[...]

    return kernel_call(
        body,
        [
            jax.ShapeDtypeStruct((rows * parts, width), pieces[0].dtype),
            jax.ShapeDtypeStruct((1 + len(others), rows * parts, width), pieces[0].dtype),
        ],
    )(*pieces, *others)


def join_columns(pieces, axis):
    rows, piece = pieces[0].shape
    parts = len(pieces)

    def body(*refs):
        copies = [
            pltpu.make_async_copy(
                refs[k], refs[parts].at[:, columns_of(axis, k, piece)], refs[parts + 1].at[k]
            )
            for k in range(parts)
        ]
        for copy in copies:
            copy.start()
        for copy in copies:
            copy.wait()

    return kernel_call(
        body,
        jax.ShapeDtypeStruct((rows, piece * parts), pieces[0].dtype),
        in_specs=[pl.BlockSpec(memory_space=pl.ANY)] * parts,
        out_specs=pl.BlockSpec(memory_space=pl.ANY),
        scratch_shapes=[pltpu.SemaphoreType.DMA((parts,))],
    )(*pieces)


def split_sum(x, y, parts):
    kinds, count, *rest = x.shape
    part = count // parts

    def body(x_ref, y_ref, *outs):
        for k in range(parts):
            here = slice(k * part, (k + 1) * part)
            outs[k][...] = x_ref[:, here] + y_ref[:, here]

    return kernel_call(body, [jax.ShapeDtypeStruct((kinds, part, *rest), x.dtype)] * parts)(x, y)


def square_sums(queries, keys):
    rows, width = queries.shape

    def body(q_ref, k_ref, out_ref):
        for i, ref in enumerate((q_ref, k_ref)):
            wide = ref[...].astype(jnp.float32)
            out_ref[:, i : i + 1] = jnp.sum(wide * wide, axis=1, keepdims=True)

    return kernel_call(
        body, jax.ShapeDtypeStruct((rows, 2), jnp.float32), (4 * rows * width, 4 * rows * width, 0)
    )(queries, keys)


def context_factor(wide):
    return lax.rsqrt(jnp.mean(wide * wide, axis=1, keepdims=True) + eps)


def context_shards(keys, values, gain, width, axis, parts):
    rows = keys.shape[0]

    def body(k_ref, v_ref, gain_ref, *outs):
        wide = k_ref[...].astype(jnp.float32)
        recip = context_factor(wide)
        for k in range(parts):
            cols = columns_of(axis, k, width)
            part = k_ref[:, cols].astype(jnp.float32) * recip * gain_ref[:, cols]
            outs[k][0] = part.astype(jnp.bfloat16)
            outs[k][1] = v_ref[:, cols]

    return kernel_call(body, [jax.ShapeDtypeStruct((2, rows, width), jnp.bfloat16)] * parts)(
        keys, values, gain[None, :]
    )


def context_gradients(keys, gain, first, second, axis):
    rows, full = keys.shape
    width = first.shape[-1]

    def body(k_ref, gain_ref, first_ref, second_ref, grad_ref, values_ref, scaled):
        for k in range(full // width):
            cols = columns_of(axis, k, width)
            scaled[:, cols] = gain_ref[:, cols] * (first_ref[2 * k, 0] + second_ref[2 * k, 0])
            values_ref[:, cols] = first_ref[2 * k + 1, 0] + second_ref[2 * k + 1, 0]
        wide = k_ref[...].astype(jnp.float32)
        recip = context_factor(wide)
        inner = jnp.mean(wide * scaled[...], axis=1, keepdims=True)
        grad_ref[...] = recip * scaled[...] - wide * (recip * recip * recip) * inner

    return kernel_call(
        body,
        [jax.ShapeDtypeStruct((rows, full), jnp.float32)] * 2,
        scratch_shapes=[pltpu.VMEM((rows, full), jnp.float32)],
    )(keys, gain[None, :], first, second)


def halves(arrays):
    kinds, count, *rest = arrays[0].shape
    half = count // 2
    n = len(arrays)

    def body(*refs):
        for i in range(n):
            refs[n][i * kinds : (i + 1) * kinds] = refs[i][:, :half]
            refs[n + 1][i * kinds : (i + 1) * kinds] = refs[i][:, half:]

    return kernel_call(
        body, [jax.ShapeDtypeStruct((n * kinds, half, *rest), arrays[0].dtype)] * 2
    )(*arrays)


def norm_factor(total_refs, which, full_width):
    total = total_refs[0][:, which : which + 1]
    for ref in total_refs[1:]:
        total = total + ref[:, which : which + 1]
    return lax.rsqrt(total / full_width + eps)


def normed_turned(x, which, totals, gain, cosine, sine, full_width, axis, parts, relative):
    rows, width = x.shape
    piece = width // parts
    n_totals = len(totals)

    def body(*refs):
        x_ref, gain_ref, cos_ref, sin_ref = refs[n_totals : n_totals + 4]
        outs = refs[n_totals + 4 :]
        recip = norm_factor(refs[:n_totals], which, full_width)
        cos = cos_ref[...]
        sin = sin_ref[...]
        even = lax.broadcasted_iota(jnp.int32, cos.shape, 1) % 2 == 0
        for k in range(parts):
            for h in range(piece // HEAD_DIM):
                start = k * piece + h * HEAD_DIM
                if parts > 1 and relative:
                    start = pl.multiple_of(
                        (lax.axis_index(axis) ^ k) * piece + h * HEAD_DIM, HEAD_DIM
                    )
                cols = pl.ds(start, HEAD_DIM)
                here = slice(h * HEAD_DIM, (h + 1) * HEAD_DIM)
                normed = x_ref[:, cols].astype(jnp.float32) * recip * gain_ref[:, cols]
                other = jnp.where(
                    even, pltpu.roll(normed, HEAD_DIM - 1, 1), pltpu.roll(normed, 1, 1)
                )
                turned = (normed * cos + other * sin).astype(jnp.bfloat16)
                if relative:
                    outs[k][:, here] = turned
                else:
                    outs[0][k, :, here] = turned

    shapes = [(rows, piece)] * parts if relative else [(parts, rows, piece)]
    return kernel_call(body, [jax.ShapeDtypeStruct(sh, jnp.bfloat16) for sh in shapes])(
        *totals, x, gain[None, :], cosine, sine
    )


def attention(query, keys, values):
    rows, width = query.shape
    factor = HEAD_DIM ** (-0.5) * LOG2E
    heads = [slice(h, h + HEAD_DIM) for h in range(0, width, HEAD_DIM)]
    pairs = [x if isinstance(x, tuple) else (x, None) for x in (*keys, *values)]
    arrays = []
    for x, _ in pairs:
        if not any(x is y for y in arrays):
            arrays.append(x)
    places = [(next(i for i, y in enumerate(arrays) if y is x), at) for x, at in pairs]

    def body(q_ref, *refs):
        def part(place, cols):
            i, at = place
            return refs[i][:, cols] if at is None else refs[i][at, :, cols]

        def scores(cols):
            q = q_ref[:, cols]
            return [
                lax.dot_general(q, part(place, cols), NT, preferred_element_type=jnp.float32)
                for place in places[: len(keys)]
            ]

        following = scores(heads[0])
        for j, cols in enumerate(heads):
            current = following
            if j + 1 < len(heads):
                following = scores(heads[j + 1])
            peak = functools.reduce(
                jnp.maximum, [jnp.max(s, axis=1, keepdims=True) for s in current]
            )
            weight_sum = 0.0
            mixed = 0.0
            for s, place in zip(current, places[len(keys) :]):
                weights = jnp.exp2((s - peak) * factor)
                weight_sum = weight_sum + jnp.sum(weights, axis=1, keepdims=True)
                mixed = mixed + jnp.dot(
                    weights.astype(jnp.bfloat16),
                    part(place, cols),
                    preferred_element_type=jnp.float32,
                )
            refs[-1][:, cols] = (mixed / weight_sum).astype(jnp.bfloat16)

    return kernel_call(body, jax.ShapeDtypeStruct((rows, width), jnp.bfloat16))(query, *arrays)


def image_attention(queries, totals, gain, full_width, context, cotangent, own_count, parts):
    rows, width = queries.shape
    n_totals = len(totals)
    count = context.shape[1]
    groups = count // (own_count * parts)
    scale = HEAD_DIM ** (-0.5)

    def body(*refs):
        q_ref, gain_ref, c_ref, g_ref, out_ref, *grad_refs = refs[n_totals:]
        recip = norm_factor(refs[:n_totals], 0, full_width)
        sides = [slice(h, h + HEAD_DIM) for h in range(0, width, HEAD_DIM)]
        heads = []
        for cols in sides:
            q = (q_ref[:, cols].astype(jnp.float32) * recip * gain_ref[:, cols]).astype(jnp.bfloat16)
            scores = scale * lax.dot_general(
                c_ref[0, :, cols], q, NT, preferred_element_type=jnp.float32
            )
            grad_p = lax.dot_general(
                c_ref[1, :, cols], g_ref[:, cols], NT, preferred_element_type=jnp.float32
            )
            heads.append((q, scores, grad_p))
        rounded = []
        for q, scores, grad_p in heads:
            weights = jnp.exp(scores - jnp.max(scores, axis=0, keepdims=True))
            probs = weights / jnp.sum(weights, axis=0, keepdims=True)
            inner = jnp.sum(probs * grad_p, axis=0, keepdims=True)
            grad_s = probs * (grad_p - inner)
            rounded.append((q, probs.astype(jnp.bfloat16), grad_s.astype(jnp.bfloat16)))
        for cols, (q, low, grad_s) in zip(sides, rounded):
            out_ref[:, cols] = lax.dot_general(
                low, c_ref[1, :, cols], TN, preferred_element_type=jnp.float32
            ).astype(jnp.bfloat16)
            grad_v = jnp.dot(low, g_ref[:, cols], preferred_element_type=jnp.float32)
            grad_k = jnp.dot(grad_s, q, preferred_element_type=jnp.float32) * scale
            for i, grad in enumerate((grad_k, grad_v)):
                grad = grad.reshape(groups, parts, own_count, HEAD_DIM)
                for k in range(parts):
                    grad_refs[k][i, :, :, cols] = grad[:, k]

    return kernel_call(
        body,
        [
            jax.ShapeDtypeStruct((rows, width), jnp.bfloat16),
            *[jax.ShapeDtypeStruct((2, groups, own_count, width), jnp.float32)] * parts,
        ],
        (1000, 1000, 0),
    )(*totals, queries, gain[None, :], context, cotangent)


def per_device(
    sizes,
    queries,
    self_keys,
    self_values,
    positions,
    query_gain,
    key_gain,
    context_keys,
    context_values,
    context_gain,
    image_cotangent,
):
    n_enc, n_row, n_col = sizes
    rows, width = queries.shape
    heads = width // HEAD_DIM
    full_width = width * n_enc
    row_bits = [1 << i for i in reversed(range(n_row.bit_length() - 1))]
    parts = n_col if heads % n_col == 0 and len(row_bits) == 2 else 1

    def relay(x):
        if parts == 1:
            return x
        return lax.all_to_all(x, "col", split_axis=0, concat_axis=0, tiled=True)

    value_split = split_columns(self_values, parts)
    values_here = relay(value_split)

    own_count = context_keys.shape[0]
    context = context_shards(after(context_keys, value_split), context_values, context_gain, width, "enc", n_enc)
    context = [swap(x, "enc", n_enc, k) if k else x for k, x in enumerate(context)]
    sums = square_sums(after(queries, context[0]), self_keys)
    totals = [sums]
    bit = 1
    while bit < n_enc:
        if len(totals) > 1:
            totals = [totals[0] + totals[1]]
        totals = [totals[0], swap(totals[0], "enc", n_enc, bit)]
        bit *= 2
    cosine, sine = rope_tables(after(positions, sums))
    key_pieces = normed_turned(
        self_keys, 1, totals, key_gain, cosine, sine, full_width, "col", parts, True
    )
    context = jnp.concatenate(context, axis=1)
    others = [0]
    for bit in row_bits:
        others += [k ^ bit for k in others]
    context = [after(swap(context, "row", n_row, k), key_pieces[0]) if k else context for k in others]
    context = jnp.concatenate(context, axis=1)
    key_pieces = [swap(x, "col", n_col, k) if k else x for k, x in enumerate(key_pieces)]

    image_out, *grads = image_attention(
        queries, totals, query_gain, full_width, context, image_cotangent, own_count, n_enc
    )

    values_here = after(values_here, grads[0]).reshape(parts * rows, width // parts)
    all_values = [values_here]
    if parts > 1:
        all_values += [swap(values_here, "row", n_row, row_bits[0])]
    grad, sent = halves([swap(x, "enc", n_enc, k) if k else x for k, x in enumerate(grads)])
    query_here = normed_turned(
        after(queries, values_here), 0, totals, query_gain, cosine, sine, full_width, "col", parts, True
    )
    key_pieces = [key_pieces[0], *(after(x, values_here, sent, *query_here) for x in key_pieces[1:])]
    keys_here, bundle = join_rows(key_pieces, all_values, "col")
    got = keys_here
    if parts > 1:
        keys_there = swap(keys_here, "row", n_row, row_bits[0])
        query_here = [swap(x, "col", n_col, k) if k else x for k, x in enumerate(query_here)]
        across = swap(bundle, "row", n_row, row_bits[1])
        all_values += [(across, 1), (across, 2)]
        all_keys = [keys_here, keys_there, (across, 0)]
        got = across
    else:
        all_keys = [lax.all_gather(keys_here, ("row", "col"), axis=0, tiled=True)]
        all_values = [lax.all_gather(values_here, ("row", "col"), axis=0, tiled=True)]

    for i in range(len(row_bits)):
        if i + 1 < len(row_bits):
            grad, sent = split_sum(grad, swap(sent, "row", n_row, 1 << i), 2)
        else:
            grad = split_sum(grad, swap(after(sent, got), "row", n_row, 1 << i), 1)[0]
    if parts > 1:
        keys_there = after(keys_there, grad, across, *query_here)
        all_keys += [swap(keys_there, "row", n_row, row_bits[1])]

    mixed = [None] * parts
    col_bits = [1 << i for i in reversed(range(n_col.bit_length() - 1))]
    for bit in col_bits[:-2]:
        grad = split_sum(grad, swap(grad, "col", n_col, bit), 1)[0]
    steps = col_bits[-2:]
    got = swap(grad, "col", n_col, steps[0])
    for i, k in enumerate(reversed(range(parts))):
        piece = attention(query_here[k], all_keys, all_values)
        mixed[k] = swap(piece, "col", n_col, k) if k else piece
        if i == 0:
            got = after(got, piece)
    if len(steps) > 1:
        grad = split_sum(grad, got, 1)[0]
        got = swap(grad, "col", n_col, steps[1])
    self_out = join_columns(mixed, "col") if parts > 1 else mixed[0]
    got = after(got, self_out)
    grad_keys_in, grad_values_in = context_gradients(context_keys, context_gain, grad, got, "enc")

    return (self_out, image_out, grad_keys_in, grad_values_in)


def solution(mesh):
    sizes = tuple(mesh.shape[a] for a in ("enc", "row", "col"))
    return jax.shard_map(
        functools.partial(per_device, sizes),
        mesh=mesh,
        in_specs=(
            P(("row", "col"), "enc"),
            P(("row", "col"), "enc"),
            P(("row", "col"), "enc"),
            P(("row", "col"), None),
            P("enc"),
            P("enc"),
            P(("enc", "row"), None),
            P(("enc", "row"), None),
            P(),
            P(("row", "col"), "enc"),
        ),
        out_specs=(
            P(("row", "col"), "enc"),
            P(("row", "col"), "enc"),
            P(("enc", "row"), None),
            P(("enc", "row"), None),
        ),
        check_vma=False,
    )
```

```python
import functools
import math

import jax
import jax.numpy as jnp
import numpy as np
from jax import lax
from jax.experimental import pallas as pl
from jax.experimental.pallas import tpu as pltpu
from jax.sharding import PartitionSpec as P

HEAD_DIM = 128
eps = 1e-06
LOG2E = 1.4426950408889634
NT = (((1,), (1,)), ((), ()))
TN = (((0,), (0,)), ((), ()))
VMEM_LIMIT = 20 * 1024 * 1024


def swap(x, axis, size, k):
    return lax.ppermute(x, axis, [(i, i ^ k) for i in range(size)])


def after(x, *others):
    return lax.optimization_barrier((x, *others))[0]


def kernel_call(body, out_shape, cost=(0, 0, 0), vmem=VMEM_LIMIT, **kw):
    return pl.pallas_call(
        body,
        out_shape=out_shape,
        compiler_params=pltpu.CompilerParams(vmem_limit_bytes=vmem),
        cost_estimate=pl.CostEstimate(flops=cost[0], bytes_accessed=cost[1], transcendentals=cost[2]),
        **kw,
    )


def rope_tables(positions):
    half = HEAD_DIM // 2
    part_side = HEAD_DIM // 6
    part_time = half - 2 * part_side
    freq_time = 1.0 / 10000.0 ** (jnp.arange(part_time, dtype=jnp.float32) * 2.0 / (2 * part_time))
    freq_side = 1.0 / 10000.0 ** (jnp.arange(part_side, dtype=jnp.float32) * 2.0 / (2 * part_side))
    freq = jnp.repeat(jnp.concatenate([freq_time, freq_side, freq_side]), 2)
    pair = np.arange(HEAD_DIM) // 2
    coords = positions.astype(jnp.float32)
    coord = jnp.where(
        pair < part_time,
        coords[:, 0:1],
        jnp.where(pair < part_time + part_side, coords[:, 1:2], coords[:, 2:3]),
    )
    angles = coord * freq
    sign = np.where(np.arange(HEAD_DIM) % 2 == 0, -1.0, 1.0).astype(np.float32)
    return jnp.cos(angles), jnp.sin(angles) * sign


def columns_of(axis, k, width):
    start = (lax.axis_index(axis) ^ k) * width
    return pl.ds(pl.multiple_of(start, HEAD_DIM), width)


def split_columns(x, parts):
    rows, width = x.shape
    piece = width // parts

    def body(x_ref, out_ref):
        for z in range(parts):
            out_ref[z] = x_ref[:, z * piece : (z + 1) * piece]

    return kernel_call(body, jax.ShapeDtypeStruct((parts, rows, piece), x.dtype))(x)


def join_rows(pieces, axis):
    rows, width = pieces[0].shape
    parts = len(pieces)

    def body(*refs):
        for k in range(parts):
            start = (lax.axis_index(axis) ^ k) * rows if parts > 1 else 0
            refs[parts][pl.ds(pl.multiple_of(start, math.gcd(rows, 32)), rows), :] = refs[k][...]

    return kernel_call(body, jax.ShapeDtypeStruct((rows * parts, width), pieces[0].dtype))(*pieces)


def join_columns(pieces, axis):
    rows, piece = pieces[0].shape
    parts = len(pieces)

    def body(*refs):
        copies = [
            pltpu.make_async_copy(
                refs[parts - 1 - k], refs[parts].at[:, columns_of(axis, k, piece)], refs[parts + 1].at[k]
            )
            for k in range(parts)
        ]
        for copy in copies:
            copy.start()
        for copy in copies:
            copy.wait()

    return kernel_call(
        body,
        jax.ShapeDtypeStruct((rows, piece * parts), pieces[0].dtype),
        in_specs=[pl.BlockSpec(memory_space=pl.ANY)] * parts,
        out_specs=pl.BlockSpec(memory_space=pl.ANY),
        scratch_shapes=[pltpu.SemaphoreType.DMA((parts,))],
    )(*pieces[::-1])


def split_sum(x, y, parts):
    kinds, count, *rest = x.shape
    part = count // parts

    def body(x_ref, y_ref, *outs):
        for k in range(parts):
            here = slice(k * part, (k + 1) * part)
            outs[k][...] = x_ref[:, here] + y_ref[:, here]

    return kernel_call(body, [jax.ShapeDtypeStruct((kinds, part, *rest), x.dtype)] * parts)(x, y)


def square_sums(queries, keys):
    rows, width = queries.shape

    def body(q_ref, k_ref, out_ref):
        for i, ref in enumerate((q_ref, k_ref)):
            wide = ref[...].astype(jnp.float32)
            out_ref[:, i : i + 1] = jnp.sum(wide * wide, axis=1, keepdims=True)

    return kernel_call(
        body, jax.ShapeDtypeStruct((rows, 2), jnp.float32), (4 * rows * width, 4 * rows * width, 0)
    )(queries, keys)


def context_factor(wide):
    return lax.rsqrt(jnp.mean(wide * wide, axis=1, keepdims=True) + eps)


def context_shards(keys, values, gain, width, axis, parts):
    rows = keys.shape[0]

    def body(k_ref, v_ref, gain_ref, *outs):
        wide = k_ref[...].astype(jnp.float32)
        recip = context_factor(wide)
        for k in range(parts):
            cols = columns_of(axis, k, width)
            part = k_ref[:, cols].astype(jnp.float32) * recip * gain_ref[:, cols]
            outs[k][0] = part.astype(jnp.bfloat16)
            outs[k][1] = v_ref[:, cols]

    return kernel_call(body, [jax.ShapeDtypeStruct((2, rows, width), jnp.bfloat16)] * parts)(
        keys, values, gain[None, :]
    )


def context_gradients(keys, gain, first, second, axis):
    rows, full = keys.shape
    width = first.shape[-1]

    def body(k_ref, gain_ref, first_ref, second_ref, grad_ref, values_ref, scaled):
        for k in range(full // width):
            cols = columns_of(axis, k, width)
            scaled[:, cols] = gain_ref[:, cols] * (first_ref[2 * k, 0] + second_ref[2 * k, 0])
            values_ref[:, cols] = first_ref[2 * k + 1, 0] + second_ref[2 * k + 1, 0]
        wide = k_ref[...].astype(jnp.float32)
        recip = context_factor(wide)
        inner = jnp.mean(wide * scaled[...], axis=1, keepdims=True)
        grad_ref[...] = recip * scaled[...] - wide * (recip * recip * recip) * inner

    return kernel_call(
        body,
        [jax.ShapeDtypeStruct((rows, full), jnp.float32)] * 2,
        scratch_shapes=[pltpu.VMEM((rows, full), jnp.float32)],
    )(keys, gain[None, :], first, second)


def halves(arrays):
    kinds, count, *rest = arrays[0].shape
    half = count // 2
    n = len(arrays)

    def body(*refs):
        for i in range(n):
            refs[n][i * kinds : (i + 1) * kinds] = refs[i][:, :half]
            refs[n + 1][i * kinds : (i + 1) * kinds] = refs[i][:, half:]

    return kernel_call(
        body, [jax.ShapeDtypeStruct((n * kinds, half, *rest), arrays[0].dtype)] * 2
    )(*arrays)


def norm_factor(total_refs, which, full_width):
    total = total_refs[0][:, which : which + 1]
    for ref in total_refs[1:]:
        total = total + ref[:, which : which + 1]
    return lax.rsqrt(total / full_width + eps)


def normed_turned(x, which, totals, gain, cosine, sine, full_width, axis, parts, relative):
    rows, width = x.shape
    piece = width // parts
    n_totals = len(totals)

    def body(*refs):
        x_ref, gain_ref, cos_ref, sin_ref = refs[n_totals : n_totals + 4]
        outs = refs[n_totals + 4 :]
        recip = norm_factor(refs[:n_totals], which, full_width)
        cos = cos_ref[...]
        sin = sin_ref[...]
        even = lax.broadcasted_iota(jnp.int32, cos.shape, 1) % 2 == 0
        for k in range(parts):
            for h in range(piece // HEAD_DIM):
                start = k * piece + h * HEAD_DIM
                if parts > 1 and relative:
                    start = pl.multiple_of(
                        (lax.axis_index(axis) ^ k) * piece + h * HEAD_DIM, HEAD_DIM
                    )
                cols = pl.ds(start, HEAD_DIM)
                here = slice(h * HEAD_DIM, (h + 1) * HEAD_DIM)
                normed = x_ref[:, cols].astype(jnp.float32) * recip * gain_ref[:, cols]
                other = jnp.where(
                    even, pltpu.roll(normed, HEAD_DIM - 1, 1), pltpu.roll(normed, 1, 1)
                )
                turned = (normed * cos + other * sin).astype(jnp.bfloat16)
                if relative:
                    outs[k][:, here] = turned
                else:
                    outs[0][k, :, here] = turned

    shapes = [(rows, piece)] * parts if relative else [(parts, rows, piece)]
    return kernel_call(body, [jax.ShapeDtypeStruct(sh, jnp.bfloat16) for sh in shapes])(
        *totals, x, gain[None, :], cosine, sine
    )


def attention(query, keys, values):
    rows, width = query.shape
    factor = HEAD_DIM ** (-0.5) * LOG2E
    heads = [slice(h, h + HEAD_DIM) for h in range(0, width, HEAD_DIM)]
    pairs = [x if isinstance(x, tuple) else (x, None) for x in (*keys, *values)]
    arrays = []
    for x, _ in pairs:
        if not any(x is y for y in arrays):
            arrays.append(x)
    places = [(next(i for i, y in enumerate(arrays) if y is x), at) for x, at in pairs]

    def body(q_ref, *refs):
        def part(place, cols):
            i, at = place
            return refs[i][:, cols] if at is None else refs[i][at, :, cols]

        def scores(cols):
            q = q_ref[:, cols]
            return [
                lax.dot_general(q, part(place, cols), NT, preferred_element_type=jnp.float32)
                for place in places[: len(keys)]
            ]

        following = scores(heads[0])
        for j, cols in enumerate(heads):
            current = following
            if j + 1 < len(heads):
                following = scores(heads[j + 1])
            peak = functools.reduce(
                jnp.maximum, [jnp.max(s, axis=1, keepdims=True) for s in current]
            )
            weight_sum = 0.0
            mixed = 0.0
            for s, place in zip(current, places[len(keys) :]):
                weights = jnp.exp2((s - peak) * factor)
                weight_sum = weight_sum + jnp.sum(weights, axis=1, keepdims=True)
                mixed = mixed + jnp.dot(
                    weights.astype(jnp.bfloat16),
                    part(place, cols),
                    preferred_element_type=jnp.float32,
                )
            refs[-1][:, cols] = (mixed / weight_sum).astype(jnp.bfloat16)

    return kernel_call(body, jax.ShapeDtypeStruct((rows, width), jnp.bfloat16))(query, *arrays)


def image_attention(queries, totals, gain, full_width, context, cotangent, own_count, parts):
    rows, width = queries.shape
    n_totals = len(totals)
    count = context.shape[1]
    groups = count // (own_count * parts)
    scale = HEAD_DIM ** (-0.5)

    def body(*refs):
        q_ref, gain_ref, c_ref, g_ref, out_ref, *grad_refs = refs[n_totals:]
        recip = norm_factor(refs[:n_totals], 0, full_width)
        sides = [slice(h, h + HEAD_DIM) for h in range(0, width, HEAD_DIM)]
        heads = []
        for cols in sides:
            q = (q_ref[:, cols].astype(jnp.float32) * recip * gain_ref[:, cols]).astype(jnp.bfloat16)
            scores = scale * lax.dot_general(
                c_ref[0, :, cols], q, NT, preferred_element_type=jnp.float32
            )
            grad_p = lax.dot_general(
                c_ref[1, :, cols], g_ref[:, cols], NT, preferred_element_type=jnp.float32
            )
            heads.append((q, scores, grad_p))
        rounded = []
        for q, scores, grad_p in heads:
            weights = jnp.exp(scores - jnp.max(scores, axis=0, keepdims=True))
            probs = weights / jnp.sum(weights, axis=0, keepdims=True)
            inner = jnp.sum(probs * grad_p, axis=0, keepdims=True)
            grad_s = probs * (grad_p - inner)
            rounded.append((q, probs.astype(jnp.bfloat16), grad_s.astype(jnp.bfloat16)))
        for cols, (q, low, grad_s) in zip(sides, rounded):
            out_ref[:, cols] = lax.dot_general(
                low, c_ref[1, :, cols], TN, preferred_element_type=jnp.float32
            ).astype(jnp.bfloat16)
            grad_v = jnp.dot(low, g_ref[:, cols], preferred_element_type=jnp.float32)
            grad_k = jnp.dot(grad_s, q, preferred_element_type=jnp.float32) * scale
            for i, grad in enumerate((grad_k, grad_v)):
                grad = grad.reshape(groups, parts, own_count, HEAD_DIM)
                for k in range(parts):
                    grad_refs[k][i, :, :, cols] = grad[:, k]

    return kernel_call(
        body,
        [
            jax.ShapeDtypeStruct((rows, width), jnp.bfloat16),
            *[jax.ShapeDtypeStruct((2, groups, own_count, width), jnp.float32)] * parts,
        ],
        (1000, 1000, 0),
    )(*totals, queries, gain[None, :], context, cotangent)


def per_device(
    sizes,
    queries,
    self_keys,
    self_values,
    positions,
    query_gain,
    key_gain,
    context_keys,
    context_values,
    context_gain,
    image_cotangent,
):
    n_enc, n_row, n_col = sizes
    rows, width = queries.shape
    heads = width // HEAD_DIM
    full_width = width * n_enc
    row_bits = [1 << i for i in reversed(range(n_row.bit_length() - 1))]
    parts = n_col if heads % n_col == 0 and len(row_bits) == 2 else 1

    def relay(x):
        if parts == 1:
            return x
        return lax.all_to_all(x, "col", split_axis=0, concat_axis=0, tiled=True)

    value_split = split_columns(self_values, parts)
    values_here = relay(value_split)

    own_count = context_keys.shape[0]
    context = context_shards(after(context_keys, value_split), context_values, context_gain, width, "enc", n_enc)
    context = [swap(x, "enc", n_enc, k) if k else x for k, x in enumerate(context)]
    sums = square_sums(after(queries, context[0]), self_keys)
    totals = [sums]
    bit = 1
    while bit < n_enc:
        if len(totals) > 1:
            totals = [totals[0] + totals[1]]
        totals = [totals[0], swap(totals[0], "enc", n_enc, bit)]
        bit *= 2
    cosine, sine = rope_tables(after(positions, sums))
    key_pieces = normed_turned(
        self_keys, 1, totals, key_gain, cosine, sine, full_width, "col", parts, True
    )
    context = jnp.concatenate(context, axis=1)
    others = [0]
    for bit in row_bits:
        others += [k ^ bit for k in others]
    context = [after(swap(context, "row", n_row, k), key_pieces[0]) if k else context for k in others]
    context = jnp.concatenate(context, axis=1)
    key_pieces = [swap(x, "col", n_col, k) if k else x for k, x in enumerate(key_pieces)]

    image_out, *grads = image_attention(
        queries, totals, query_gain, full_width, context, image_cotangent, own_count, n_enc
    )

    values_here = after(values_here, grads[0]).reshape(parts * rows, width // parts)
    all_values = [values_here]
    if parts > 1:
        all_values += [swap(values_here, "row", n_row, row_bits[0])]
    grad, sent = halves([swap(x, "enc", n_enc, k) if k else x for k, x in enumerate(grads)])
    query_here = normed_turned(
        after(queries, values_here), 0, totals, query_gain, cosine, sine, full_width, "col", parts, True
    )
    key_pieces = [
        key_pieces[0], *(after(x, all_values[-1], sent, *query_here) for x in key_pieces[1:])
    ]
    keys_here = join_rows(key_pieces, "col")
    got = keys_here
    if parts > 1:
        keys_there = swap(keys_here, "row", n_row, row_bits[0])
        query_here = [swap(x, "col", n_col, k) if k else x for k, x in enumerate(query_here)]
        all_values += [swap(x, "row", n_row, row_bits[1]) for x in all_values]
        all_keys = [keys_here, keys_there, swap(keys_here, "row", n_row, row_bits[1])]
    else:
        all_keys = [lax.all_gather(keys_here, ("row", "col"), axis=0, tiled=True)]
        all_values = [lax.all_gather(values_here, ("row", "col"), axis=0, tiled=True)]

    for i in range(len(row_bits)):
        if i + 1 < len(row_bits):
            grad, sent = split_sum(grad, swap(sent, "row", n_row, 1 << i), 2)
        else:
            grad = split_sum(grad, swap(after(sent, got), "row", n_row, 1 << i), 1)[0]
    if parts > 1:
        keys_there = after(keys_there, grad, *query_here)
        all_keys += [swap(keys_there, "row", n_row, row_bits[1])]

    mixed = [None] * parts
    col_bits = [1 << i for i in reversed(range(n_col.bit_length() - 1))]
    for bit in col_bits[:-2]:
        grad = split_sum(grad, swap(grad, "col", n_col, bit), 1)[0]
    steps = col_bits[-2:]
    got = swap(grad, "col", n_col, steps[0])
    for i, k in enumerate(reversed(range(parts))):
        piece = attention(query_here[k], all_keys, all_values)
        mixed[k] = swap(piece, "col", n_col, k) if k else piece
        if i == 0:
            got = after(got, piece)
    if len(steps) > 1:
        grad = split_sum(grad, got, 1)[0]
        got = swap(grad, "col", n_col, steps[1])
    self_out = join_columns(mixed, "col") if parts > 1 else mixed[0]
    got = after(got, self_out)
    grad_keys_in, grad_values_in = context_gradients(context_keys, context_gain, grad, got, "enc")

    return (self_out, image_out, grad_keys_in, grad_values_in)


def solution(mesh):
    sizes = tuple(mesh.shape[a] for a in ("enc", "row", "col"))
    return jax.shard_map(
        functools.partial(per_device, sizes),
        mesh=mesh,
        in_specs=(
            P(("row", "col"), "enc"),
            P(("row", "col"), "enc"),
            P(("row", "col"), "enc"),
            P(("row", "col"), None),
            P("enc"),
            P("enc"),
            P(("enc", "row"), None),
            P(("enc", "row"), None),
            P(),
            P(("row", "col"), "enc"),
        ),
        out_specs=(
            P(("row", "col"), "enc"),
            P(("row", "col"), "enc"),
            P(("enc", "row"), None),
            P(("enc", "row"), None),
        ),
        check_vma=False,
    )
```

```python
import functools
import math

import jax
import jax.numpy as jnp
import numpy as np
from jax import lax
from jax.experimental import pallas as pl
from jax.experimental.pallas import tpu as pltpu
from jax.sharding import PartitionSpec as P

HEAD_DIM = 128
eps = 1e-06
LOG2E = 1.4426950408889634
NT = (((1,), (1,)), ((), ()))
TN = (((0,), (0,)), ((), ()))
VMEM_LIMIT = 20 * 1024 * 1024


def swap(x, axis, size, k):
    return lax.ppermute(x, axis, [(i, i ^ k) for i in range(size)])


def after(x, *others):
    return lax.optimization_barrier((x, *others))[0]


def kernel_call(body, out_shape, cost=(0, 0, 0), vmem=VMEM_LIMIT, **kw):
    return pl.pallas_call(
        body,
        out_shape=out_shape,
        compiler_params=pltpu.CompilerParams(vmem_limit_bytes=vmem),
        cost_estimate=pl.CostEstimate(flops=cost[0], bytes_accessed=cost[1], transcendentals=cost[2]),
        **kw,
    )


def rope_tables(positions):
    half = HEAD_DIM // 2
    part_side = HEAD_DIM // 6
    part_time = half - 2 * part_side
    freq_time = 1.0 / 10000.0 ** (jnp.arange(part_time, dtype=jnp.float32) * 2.0 / (2 * part_time))
    freq_side = 1.0 / 10000.0 ** (jnp.arange(part_side, dtype=jnp.float32) * 2.0 / (2 * part_side))
    freq = jnp.repeat(jnp.concatenate([freq_time, freq_side, freq_side]), 2)
    pair = np.arange(HEAD_DIM) // 2
    coords = positions.astype(jnp.float32)
    coord = jnp.where(
        pair < part_time,
        coords[:, 0:1],
        jnp.where(pair < part_time + part_side, coords[:, 1:2], coords[:, 2:3]),
    )
    angles = coord * freq
    sign = np.where(np.arange(HEAD_DIM) % 2 == 0, -1.0, 1.0).astype(np.float32)
    return jnp.cos(angles), jnp.sin(angles) * sign


def columns_of(axis, k, width):
    start = (lax.axis_index(axis) ^ k) * width
    return pl.ds(pl.multiple_of(start, HEAD_DIM), width)


def split_columns(x, parts):
    rows, width = x.shape
    piece = width // parts

    def body(x_ref, out_ref):
        for z in range(parts):
            out_ref[z] = x_ref[:, z * piece : (z + 1) * piece]

    return kernel_call(body, jax.ShapeDtypeStruct((parts, rows, piece), x.dtype))(x)


def join_rows(pieces, axis):
    rows, width = pieces[0].shape
    parts = len(pieces)

    def body(*refs):
        for k in range(parts):
            start = (lax.axis_index(axis) ^ k) * rows if parts > 1 else 0
            refs[parts][pl.ds(pl.multiple_of(start, math.gcd(rows, 32)), rows), :] = refs[parts - 1 - k][...]

    return kernel_call(body, jax.ShapeDtypeStruct((rows * parts, width), pieces[0].dtype))(*pieces[::-1])


def join_columns(pieces, axis):
    rows, piece = pieces[0].shape
    parts = len(pieces)

    def body(*refs):
        copies = [
            pltpu.make_async_copy(
                refs[parts - 1 - k], refs[parts].at[:, columns_of(axis, k, piece)], refs[parts + 1].at[k]
            )
            for k in range(parts)
        ]
        for copy in copies:
            copy.start()
        for copy in copies:
            copy.wait()

    return kernel_call(
        body,
        jax.ShapeDtypeStruct((rows, piece * parts), pieces[0].dtype),
        in_specs=[pl.BlockSpec(memory_space=pl.ANY)] * parts,
        out_specs=pl.BlockSpec(memory_space=pl.ANY),
        scratch_shapes=[pltpu.SemaphoreType.DMA((parts,))],
    )(*pieces[::-1])


def split_sum(x, y, parts):
    kinds, count, *rest = x.shape
    part = count // parts

    def body(x_ref, y_ref, *outs):
        for k in range(parts):
            here = slice(k * part, (k + 1) * part)
            outs[k][...] = x_ref[:, here] + y_ref[:, here]

    return kernel_call(body, [jax.ShapeDtypeStruct((kinds, part, *rest), x.dtype)] * parts)(x, y)


def square_sums(queries, keys):
    rows, width = queries.shape

    def body(q_ref, k_ref, out_ref):
        for i, ref in enumerate((q_ref, k_ref)):
            wide = ref[...].astype(jnp.float32)
            out_ref[:, i : i + 1] = jnp.sum(wide * wide, axis=1, keepdims=True)

    return kernel_call(
        body, jax.ShapeDtypeStruct((rows, 2), jnp.float32), (4 * rows * width, 4 * rows * width, 0)
    )(queries, keys)


def context_factor(wide):
    return lax.rsqrt(jnp.mean(wide * wide, axis=1, keepdims=True) + eps)


def context_shards(keys, values, gain, width, axis, parts):
    rows = keys.shape[0]

    def body(k_ref, v_ref, gain_ref, *outs):
        wide = k_ref[...].astype(jnp.float32)
        recip = context_factor(wide)
        for k in range(parts):
            cols = columns_of(axis, k, width)
            part = k_ref[:, cols].astype(jnp.float32) * recip * gain_ref[:, cols]
            outs[k][0] = part.astype(jnp.bfloat16)
            outs[k][1] = v_ref[:, cols]

    return kernel_call(body, [jax.ShapeDtypeStruct((2, rows, width), jnp.bfloat16)] * parts)(
        keys, values, gain[None, :]
    )


def context_gradients(keys, gain, first, second, axis):
    rows, full = keys.shape
    width = first.shape[-1]

    def body(k_ref, gain_ref, first_ref, second_ref, grad_ref, values_ref, scaled):
        for k in range(full // width):
            cols = columns_of(axis, k, width)
            scaled[:, cols] = gain_ref[:, cols] * (first_ref[2 * k, 0] + second_ref[2 * k, 0])
            values_ref[:, cols] = first_ref[2 * k + 1, 0] + second_ref[2 * k + 1, 0]
        wide = k_ref[...].astype(jnp.float32)
        recip = context_factor(wide)
        inner = jnp.mean(wide * scaled[...], axis=1, keepdims=True)
        grad_ref[...] = recip * scaled[...] - wide * (recip * recip * recip) * inner

    return kernel_call(
        body,
        [jax.ShapeDtypeStruct((rows, full), jnp.float32)] * 2,
        scratch_shapes=[pltpu.VMEM((rows, full), jnp.float32)],
    )(keys, gain[None, :], first, second)


def halves(arrays):
    kinds, count, *rest = arrays[0].shape
    half = count // 2
    n = len(arrays)

    def body(*refs):
        for i in range(n):
            refs[n][i * kinds : (i + 1) * kinds] = refs[i][:, :half]
            refs[n + 1][i * kinds : (i + 1) * kinds] = refs[i][:, half:]

    return kernel_call(
        body, [jax.ShapeDtypeStruct((n * kinds, half, *rest), arrays[0].dtype)] * 2
    )(*arrays)


def norm_factor(total_refs, which, full_width):
    total = total_refs[0][:, which : which + 1]
    for ref in total_refs[1:]:
        total = total + ref[:, which : which + 1]
    return lax.rsqrt(total / full_width + eps)


def normed_turned(x, which, totals, gain, cosine, sine, full_width, axis, parts, relative):
    rows, width = x.shape
    piece = width // parts
    n_totals = len(totals)

    def body(*refs):
        x_ref, gain_ref, cos_ref, sin_ref = refs[n_totals : n_totals + 4]
        outs = refs[n_totals + 4 :]
        recip = norm_factor(refs[:n_totals], which, full_width)
        cos = cos_ref[...]
        sin = sin_ref[...]
        even = lax.broadcasted_iota(jnp.int32, cos.shape, 1) % 2 == 0
        for k in range(parts):
            for h in range(piece // HEAD_DIM):
                start = k * piece + h * HEAD_DIM
                if parts > 1 and relative:
                    start = pl.multiple_of(
                        (lax.axis_index(axis) ^ k) * piece + h * HEAD_DIM, HEAD_DIM
                    )
                cols = pl.ds(start, HEAD_DIM)
                here = slice(h * HEAD_DIM, (h + 1) * HEAD_DIM)
                normed = x_ref[:, cols].astype(jnp.float32) * recip * gain_ref[:, cols]
                other = jnp.where(
                    even, pltpu.roll(normed, HEAD_DIM - 1, 1), pltpu.roll(normed, 1, 1)
                )
                turned = (normed * cos + other * sin).astype(jnp.bfloat16)
                if relative:
                    outs[k][:, here] = turned
                else:
                    outs[0][k, :, here] = turned

    shapes = [(rows, piece)] * parts if relative else [(parts, rows, piece)]
    return kernel_call(body, [jax.ShapeDtypeStruct(sh, jnp.bfloat16) for sh in shapes])(
        *totals, x, gain[None, :], cosine, sine
    )


def attention(query, keys, values):
    rows, width = query.shape
    factor = HEAD_DIM ** (-0.5) * LOG2E
    heads = [slice(h, h + HEAD_DIM) for h in range(0, width, HEAD_DIM)]
    pairs = [x if isinstance(x, tuple) else (x, None) for x in (*keys, *values)]
    arrays = []
    for x, _ in pairs:
        if not any(x is y for y in arrays):
            arrays.append(x)
    places = [(next(i for i, y in enumerate(arrays) if y is x), at) for x, at in pairs]

    def body(q_ref, *refs):
        def part(place, cols):
            i, at = place
            return refs[i][:, cols] if at is None else refs[i][at, :, cols]

        def scores(cols):
            q = q_ref[:, cols]
            return [
                lax.dot_general(q, part(place, cols), NT, preferred_element_type=jnp.float32)
                for place in places[: len(keys)]
            ]

        following = scores(heads[0])
        for j, cols in enumerate(heads):
            current = following
            if j + 1 < len(heads):
                following = scores(heads[j + 1])
            peak = functools.reduce(
                jnp.maximum, [jnp.max(s, axis=1, keepdims=True) for s in current]
            )
            weight_sum = 0.0
            mixed = 0.0
            for s, place in zip(current, places[len(keys) :]):
                weights = jnp.exp2((s - peak) * factor)
                weight_sum = weight_sum + jnp.sum(weights, axis=1, keepdims=True)
                mixed = mixed + jnp.dot(
                    weights.astype(jnp.bfloat16),
                    part(place, cols),
                    preferred_element_type=jnp.float32,
                )
            refs[-1][:, cols] = (mixed / weight_sum).astype(jnp.bfloat16)

    return kernel_call(body, jax.ShapeDtypeStruct((rows, width), jnp.bfloat16))(query, *arrays)


def image_attention(queries, totals, gain, full_width, context, cotangent, own_count, parts):
    rows, width = queries.shape
    n_totals = len(totals)
    count = context.shape[1]
    groups = count // (own_count * parts)
    scale = HEAD_DIM ** (-0.5)

    def body(*refs):
        q_ref, gain_ref, c_ref, g_ref, out_ref, *grad_refs = refs[n_totals:]
        recip = norm_factor(refs[:n_totals], 0, full_width)
        sides = [slice(h, h + HEAD_DIM) for h in range(0, width, HEAD_DIM)]
        heads = []
        for cols in sides:
            q = (q_ref[:, cols].astype(jnp.float32) * recip * gain_ref[:, cols]).astype(jnp.bfloat16)
            scores = scale * lax.dot_general(
                c_ref[0, :, cols], q, NT, preferred_element_type=jnp.float32
            )
            grad_p = lax.dot_general(
                c_ref[1, :, cols], g_ref[:, cols], NT, preferred_element_type=jnp.float32
            )
            heads.append((q, scores, grad_p))
        rounded = []
        for q, scores, grad_p in heads:
            weights = jnp.exp(scores - jnp.max(scores, axis=0, keepdims=True))
            probs = weights / jnp.sum(weights, axis=0, keepdims=True)
            inner = jnp.sum(probs * grad_p, axis=0, keepdims=True)
            grad_s = probs * (grad_p - inner)
            rounded.append((q, probs.astype(jnp.bfloat16), grad_s.astype(jnp.bfloat16)))
        for cols, (q, low, grad_s) in zip(sides, rounded):
            out_ref[:, cols] = lax.dot_general(
                low, c_ref[1, :, cols], TN, preferred_element_type=jnp.float32
            ).astype(jnp.bfloat16)
            grad_v = jnp.dot(low, g_ref[:, cols], preferred_element_type=jnp.float32)
            grad_k = jnp.dot(grad_s, q, preferred_element_type=jnp.float32) * scale
            for i, grad in enumerate((grad_k, grad_v)):
                grad = grad.reshape(groups, parts, own_count, HEAD_DIM)
                for k in range(parts):
                    grad_refs[k][i, :, :, cols] = grad[:, k]

    return kernel_call(
        body,
        [
            jax.ShapeDtypeStruct((rows, width), jnp.bfloat16),
            *[jax.ShapeDtypeStruct((2, groups, own_count, width), jnp.float32)] * parts,
        ],
        (1000, 1000, 0),
    )(*totals, queries, gain[None, :], context, cotangent)


def per_device(
    sizes,
    queries,
    self_keys,
    self_values,
    positions,
    query_gain,
    key_gain,
    context_keys,
    context_values,
    context_gain,
    image_cotangent,
):
    n_enc, n_row, n_col = sizes
    rows, width = queries.shape
    heads = width // HEAD_DIM
    full_width = width * n_enc
    row_bits = [1 << i for i in reversed(range(n_row.bit_length() - 1))]
    parts = n_col if heads % n_col == 0 and len(row_bits) == 2 else 1

    def relay(x):
        if parts == 1:
            return x
        return lax.all_to_all(x, "col", split_axis=0, concat_axis=0, tiled=True)

    value_split = split_columns(self_values, parts)
    values_here = relay(value_split)

    own_count = context_keys.shape[0]
    context = context_shards(after(context_keys, value_split), context_values, context_gain, width, "enc", n_enc)
    context = [swap(x, "enc", n_enc, k) if k else x for k, x in enumerate(context)]
    sums = square_sums(after(queries, value_split), self_keys)
    totals = [sums]
    bit = 1
    while bit < n_enc:
        if len(totals) > 1:
            totals = [totals[0] + totals[1]]
        totals = [totals[0], swap(totals[0], "enc", n_enc, bit)]
        bit *= 2
    cosine, sine = rope_tables(after(positions, value_split))
    key_pieces = normed_turned(
        self_keys, 1, totals, key_gain, cosine, sine, full_width, "col", parts, True
    )
    context = jnp.concatenate(context, axis=1)
    others = [0]
    for bit in row_bits:
        others += [k ^ bit for k in others]
    context = [after(swap(context, "row", n_row, k), key_pieces[0]) if k else context for k in others]
    context = jnp.concatenate(context, axis=1)
    key_pieces = [swap(x, "col", n_col, k) if k else x for k, x in enumerate(key_pieces)]

    image_out, *grads = image_attention(
        queries, totals, query_gain, full_width, context, image_cotangent, own_count, n_enc
    )

    values_here = after(values_here, context).reshape(parts * rows, width // parts)
    all_values = [values_here]
    if parts > 1:
        all_values += [swap(values_here, "row", n_row, row_bits[0])]
    grad, sent = halves([swap(x, "enc", n_enc, k) if k else x for k, x in enumerate(grads)])
    query_here = normed_turned(
        after(queries, values_here), 0, totals, query_gain, cosine, sine, full_width, "col", parts, True
    )
    key_pieces = [
        key_pieces[0], *(after(x, all_values[-1], *query_here) for x in key_pieces[1:])
    ]
    keys_here = join_rows(key_pieces, "col")
    got = keys_here
    if parts > 1:
        keys_there = swap(keys_here, "row", n_row, row_bits[0])
        moved = {k: swap(query_here[k], "col", n_col, k) for k in reversed(range(1, parts))}
        query_here = [query_here[0]] + [moved[k] for k in range(1, parts)]
        all_values += [swap(x, "row", n_row, row_bits[1]) for x in all_values]
        all_keys = [keys_here, keys_there, swap(keys_here, "row", n_row, row_bits[1])]
    else:
        all_keys = [lax.all_gather(keys_here, ("row", "col"), axis=0, tiled=True)]
        all_values = [lax.all_gather(values_here, ("row", "col"), axis=0, tiled=True)]

    for i in range(len(row_bits)):
        if i + 1 < len(row_bits):
            grad, sent = split_sum(grad, swap(sent, "row", n_row, 1 << i), 2)
        else:
            grad = split_sum(grad, swap(after(sent, got), "row", n_row, 1 << i), 1)[0]
    if parts > 1:
        keys_there = after(keys_there, grad, *query_here)
        all_keys += [swap(keys_there, "row", n_row, row_bits[1])]

    if parts > 1:
        all_keys = all_keys[::-1]
        all_values = all_values[::-1]

    mixed = [None] * parts
    col_bits = [1 << i for i in reversed(range(n_col.bit_length() - 1))]
    for bit in col_bits[:-2]:
        grad = split_sum(grad, swap(grad, "col", n_col, bit), 1)[0]
    steps = col_bits[-2:]
    got = swap(grad, "col", n_col, steps[0])
    for i, k in enumerate(reversed(range(parts))):
        piece = attention(query_here[k], all_keys, all_values)
        mixed[k] = swap(piece, "col", n_col, k) if k else piece
        if i == 0:
            got = after(got, piece)
    if len(steps) > 1:
        grad = split_sum(grad, got, 1)[0]
        got = swap(grad, "col", n_col, steps[1])
    self_out = join_columns(mixed, "col") if parts > 1 else mixed[0]
    got = after(got, self_out)
    grad_keys_in, grad_values_in = context_gradients(context_keys, context_gain, grad, got, "enc")

    return (self_out, image_out, grad_keys_in, grad_values_in)


def solution(mesh):
    sizes = tuple(mesh.shape[a] for a in ("enc", "row", "col"))
    return jax.shard_map(
        functools.partial(per_device, sizes),
        mesh=mesh,
        in_specs=(
            P(("row", "col"), "enc"),
            P(("row", "col"), "enc"),
            P(("row", "col"), "enc"),
            P(("row", "col"), None),
            P("enc"),
            P("enc"),
            P(("enc", "row"), None),
            P(("enc", "row"), None),
            P(),
            P(("row", "col"), "enc"),
        ),
        out_specs=(
            P(("row", "col"), "enc"),
            P(("row", "col"), "enc"),
            P(("enc", "row"), None),
            P(("enc", "row"), None),
        ),
        check_vma=False,
    )
```

```python
import functools
import math

import jax
import jax.numpy as jnp
import numpy as np
from jax import lax
from jax.experimental import pallas as pl
from jax.experimental.pallas import tpu as pltpu
from jax.sharding import PartitionSpec as P

HEAD_DIM = 128
eps = 1e-06
LOG2E = 1.4426950408889634
NT = (((1,), (1,)), ((), ()))
TN = (((0,), (0,)), ((), ()))
VMEM_LIMIT = 20 * 1024 * 1024


def swap(x, axis, size, k):
    return lax.ppermute(x, axis, [(i, i ^ k) for i in range(size)])


def after(x, *others):
    return lax.optimization_barrier((x, *others))[0]


def kernel_call(body, out_shape, cost=(0, 0, 0), vmem=VMEM_LIMIT, **kw):
    return pl.pallas_call(
        body,
        out_shape=out_shape,
        compiler_params=pltpu.CompilerParams(vmem_limit_bytes=vmem),
        cost_estimate=pl.CostEstimate(flops=cost[0], bytes_accessed=cost[1], transcendentals=cost[2]),
        **kw,
    )


def rope_tables(positions):
    half = HEAD_DIM // 2
    part_side = HEAD_DIM // 6
    part_time = half - 2 * part_side
    freq_time = 1.0 / 10000.0 ** (jnp.arange(part_time, dtype=jnp.float32) * 2.0 / (2 * part_time))
    freq_side = 1.0 / 10000.0 ** (jnp.arange(part_side, dtype=jnp.float32) * 2.0 / (2 * part_side))
    freq = jnp.repeat(jnp.concatenate([freq_time, freq_side, freq_side]), 2)
    pair = np.arange(HEAD_DIM) // 2
    coords = positions.astype(jnp.float32)
    coord = jnp.where(
        pair < part_time,
        coords[:, 0:1],
        jnp.where(pair < part_time + part_side, coords[:, 1:2], coords[:, 2:3]),
    )
    angles = coord * freq
    sign = np.where(np.arange(HEAD_DIM) % 2 == 0, -1.0, 1.0).astype(np.float32)
    return jnp.cos(angles), jnp.sin(angles) * sign


def columns_of(axis, k, width):
    start = (lax.axis_index(axis) ^ k) * width
    return pl.ds(pl.multiple_of(start, HEAD_DIM), width)


def split_columns(x, parts):
    rows, width = x.shape
    piece = width // parts

    def body(x_ref, out_ref):
        for z in range(parts):
            out_ref[z] = x_ref[:, z * piece : (z + 1) * piece]

    return kernel_call(body, jax.ShapeDtypeStruct((parts, rows, piece), x.dtype))(x)


def join_rows(pieces, axis):
    rows, width = pieces[0].shape
    parts = len(pieces)

    def body(*refs):
        for k in range(parts):
            start = (lax.axis_index(axis) ^ k) * rows if parts > 1 else 0
            refs[parts][pl.ds(pl.multiple_of(start, math.gcd(rows, 32)), rows), :] = refs[parts - 1 - k][...]

    return kernel_call(body, jax.ShapeDtypeStruct((rows * parts, width), pieces[0].dtype))(*pieces[::-1])


def join_columns(pieces, axis):
    rows, piece = pieces[0].shape
    parts = len(pieces)

    def body(*refs):
        copies = [
            pltpu.make_async_copy(
                refs[parts - 1 - k], refs[parts].at[:, columns_of(axis, k, piece)], refs[parts + 1].at[k]
            )
            for k in range(parts)
        ]
        for copy in copies:
            copy.start()
        for copy in copies:
            copy.wait()

    return kernel_call(
        body,
        jax.ShapeDtypeStruct((rows, piece * parts), pieces[0].dtype),
        in_specs=[pl.BlockSpec(memory_space=pl.ANY)] * parts,
        out_specs=pl.BlockSpec(memory_space=pl.ANY),
        scratch_shapes=[pltpu.SemaphoreType.DMA((parts,))],
    )(*pieces[::-1])


def split_sum(x, y, parts):
    kinds, count, *rest = x.shape
    part = count // parts

    def body(x_ref, y_ref, *outs):
        for k in range(parts):
            here = slice(k * part, (k + 1) * part)
            outs[k][...] = x_ref[:, here] + y_ref[:, here]

    return kernel_call(body, [jax.ShapeDtypeStruct((kinds, part, *rest), x.dtype)] * parts)(x, y)


def square_sums(queries, keys):
    rows, width = queries.shape

    def body(q_ref, k_ref, out_ref):
        for i, ref in enumerate((q_ref, k_ref)):
            wide = ref[...].astype(jnp.float32)
            out_ref[:, i : i + 1] = jnp.sum(wide * wide, axis=1, keepdims=True)

    return kernel_call(
        body, jax.ShapeDtypeStruct((rows, 2), jnp.float32), (4 * rows * width, 4 * rows * width, 0)
    )(queries, keys)


def context_factor(wide):
    return lax.rsqrt(jnp.mean(wide * wide, axis=1, keepdims=True) + eps)


def context_shards(keys, values, gain, width, axis, parts):
    rows = keys.shape[0]

    def body(k_ref, v_ref, gain_ref, *outs):
        wide = k_ref[...].astype(jnp.float32)
        recip = context_factor(wide)
        for k in range(parts):
            cols = columns_of(axis, k, width)
            part = k_ref[:, cols].astype(jnp.float32) * recip * gain_ref[:, cols]
            outs[k][0] = part.astype(jnp.bfloat16)
            outs[k][1] = v_ref[:, cols]

    return kernel_call(body, [jax.ShapeDtypeStruct((2, rows, width), jnp.bfloat16)] * parts)(
        keys, values, gain[None, :]
    )


def context_gradients(keys, gain, first, second, axis):
    rows, full = keys.shape
    width = first.shape[-1]

    def body(k_ref, gain_ref, first_ref, second_ref, grad_ref, values_ref, scaled):
        for k in range(full // width):
            cols = columns_of(axis, k, width)
            scaled[:, cols] = gain_ref[:, cols] * (first_ref[2 * k, 0] + second_ref[2 * k, 0])
            values_ref[:, cols] = first_ref[2 * k + 1, 0] + second_ref[2 * k + 1, 0]
        wide = k_ref[...].astype(jnp.float32)
        recip = context_factor(wide)
        inner = jnp.mean(wide * scaled[...], axis=1, keepdims=True)
        grad_ref[...] = recip * scaled[...] - wide * (recip * recip * recip) * inner

    return kernel_call(
        body,
        [jax.ShapeDtypeStruct((rows, full), jnp.float32)] * 2,
        scratch_shapes=[pltpu.VMEM((rows, full), jnp.float32)],
    )(keys, gain[None, :], first, second)


def halves(arrays):
    kinds, count, *rest = arrays[0].shape
    half = count // 2
    n = len(arrays)

    def body(*refs):
        for i in range(n):
            refs[n][i * kinds : (i + 1) * kinds] = refs[i][:, :half]
            refs[n + 1][i * kinds : (i + 1) * kinds] = refs[i][:, half:]

    return kernel_call(
        body, [jax.ShapeDtypeStruct((n * kinds, half, *rest), arrays[0].dtype)] * 2
    )(*arrays)


def norm_factor(total_refs, which, full_width):
    total = total_refs[0][:, which : which + 1]
    for ref in total_refs[1:]:
        total = total + ref[:, which : which + 1]
    return lax.rsqrt(total / full_width + eps)


def normed_turned(x, which, totals, gain, cosine, sine, full_width, axis, parts, relative):
    rows, width = x.shape
    piece = width // parts
    n_totals = len(totals)

    def body(*refs):
        x_ref, gain_ref, cos_ref, sin_ref = refs[n_totals : n_totals + 4]
        outs = refs[n_totals + 4 :]
        recip = norm_factor(refs[:n_totals], which, full_width)
        cos = cos_ref[...]
        sin = sin_ref[...]
        even = lax.broadcasted_iota(jnp.int32, cos.shape, 1) % 2 == 0
        for k in range(parts):
            for h in range(piece // HEAD_DIM):
                start = k * piece + h * HEAD_DIM
                if parts > 1 and relative:
                    start = pl.multiple_of(
                        (lax.axis_index(axis) ^ k) * piece + h * HEAD_DIM, HEAD_DIM
                    )
                cols = pl.ds(start, HEAD_DIM)
                here = slice(h * HEAD_DIM, (h + 1) * HEAD_DIM)
                normed = x_ref[:, cols].astype(jnp.float32) * recip * gain_ref[:, cols]
                other = jnp.where(
                    even, pltpu.roll(normed, HEAD_DIM - 1, 1), pltpu.roll(normed, 1, 1)
                )
                turned = (normed * cos + other * sin).astype(jnp.bfloat16)
                if relative:
                    outs[k][:, here] = turned
                else:
                    outs[0][k, :, here] = turned

    shapes = [(rows, piece)] * parts if relative else [(parts, rows, piece)]
    return kernel_call(body, [jax.ShapeDtypeStruct(sh, jnp.bfloat16) for sh in shapes])(
        *totals, x, gain[None, :], cosine, sine
    )


def attention(query, keys, values):
    rows, width = query.shape
    factor = HEAD_DIM ** (-0.5) * LOG2E
    heads = [slice(h, h + HEAD_DIM) for h in range(0, width, HEAD_DIM)]
    pairs = [x if isinstance(x, tuple) else (x, None) for x in (*keys, *values)]
    arrays = []
    for x, _ in pairs:
        if not any(x is y for y in arrays):
            arrays.append(x)
    places = [(next(i for i, y in enumerate(arrays) if y is x), at) for x, at in pairs]

    def body(q_ref, *refs):
        def part(place, cols):
            i, at = place
            return refs[i][:, cols] if at is None else refs[i][at, :, cols]

        def scores(cols):
            q = q_ref[:, cols]
            return [
                lax.dot_general(q, part(place, cols), NT, preferred_element_type=jnp.float32)
                for place in places[: len(keys)]
            ]

        following = scores(heads[0])
        for j, cols in enumerate(heads):
            current = following
            if j + 1 < len(heads):
                following = scores(heads[j + 1])
            peak = jnp.max(functools.reduce(jnp.maximum, current), axis=1, keepdims=True)
            weights = [jnp.exp2((s - peak) * factor) for s in current]
            weight_sum = jnp.sum(sum(weights[1:], weights[0]), axis=1, keepdims=True)
            mixed = 0.0
            for w, place in zip(weights, places[len(keys) :]):
                mixed = mixed + jnp.dot(
                    w.astype(jnp.bfloat16), part(place, cols), preferred_element_type=jnp.float32
                )
            refs[-1][:, cols] = (mixed / weight_sum).astype(jnp.bfloat16)

    return kernel_call(body, jax.ShapeDtypeStruct((rows, width), jnp.bfloat16))(query, *arrays)


def image_attention(queries, totals, gain, full_width, context, cotangent, own_count, parts):
    rows, width = queries.shape
    n_totals = len(totals)
    count = context.shape[1]
    groups = count // (own_count * parts)
    scale = HEAD_DIM ** (-0.5)

    def body(*refs):
        q_ref, gain_ref, c_ref, g_ref, out_ref, *grad_refs = refs[n_totals:]
        recip = norm_factor(refs[:n_totals], 0, full_width)
        sides = [slice(h, h + HEAD_DIM) for h in range(0, width, HEAD_DIM)]
        heads = []
        for cols in sides:
            q = (q_ref[:, cols].astype(jnp.float32) * recip * gain_ref[:, cols]).astype(jnp.bfloat16)
            scores = scale * lax.dot_general(
                c_ref[0, :, cols], q, NT, preferred_element_type=jnp.float32
            )
            grad_p = lax.dot_general(
                c_ref[1, :, cols], g_ref[:, cols], NT, preferred_element_type=jnp.float32
            )
            heads.append((q, scores, grad_p))
        rounded = []
        for q, scores, grad_p in heads:
            weights = jnp.exp(scores - jnp.max(scores, axis=0, keepdims=True))
            probs = weights / jnp.sum(weights, axis=0, keepdims=True)
            inner = jnp.sum(probs * grad_p, axis=0, keepdims=True)
            grad_s = probs * (grad_p - inner)
            rounded.append((q, probs.astype(jnp.bfloat16), grad_s.astype(jnp.bfloat16)))
        for cols, (q, low, grad_s) in zip(sides, rounded):
            out_ref[:, cols] = lax.dot_general(
                low, c_ref[1, :, cols], TN, preferred_element_type=jnp.float32
            ).astype(jnp.bfloat16)
            grad_v = jnp.dot(low, g_ref[:, cols], preferred_element_type=jnp.float32)
            grad_k = jnp.dot(grad_s, q, preferred_element_type=jnp.float32) * scale
            for i, grad in enumerate((grad_k, grad_v)):
                grad = grad.reshape(groups, parts, own_count, HEAD_DIM)
                for k in range(parts):
                    grad_refs[k][i, :, :, cols] = grad[:, k]

    return kernel_call(
        body,
        [
            jax.ShapeDtypeStruct((rows, width), jnp.bfloat16),
            *[jax.ShapeDtypeStruct((2, groups, own_count, width), jnp.float32)] * parts,
        ],
        (1000, 1000, 0),
    )(*totals, queries, gain[None, :], context, cotangent)


def per_device(
    sizes,
    queries,
    self_keys,
    self_values,
    positions,
    query_gain,
    key_gain,
    context_keys,
    context_values,
    context_gain,
    image_cotangent,
):
    n_enc, n_row, n_col = sizes
    rows, width = queries.shape
    heads = width // HEAD_DIM
    full_width = width * n_enc
    row_bits = [1 << i for i in reversed(range(n_row.bit_length() - 1))]
    parts = n_col if heads % n_col == 0 and len(row_bits) == 2 else 1

    def relay(x):
        if parts == 1:
            return x
        return lax.all_to_all(x, "col", split_axis=0, concat_axis=0, tiled=True)

    value_split = split_columns(self_values, parts)
    values_here = relay(value_split)

    own_count = context_keys.shape[0]
    context = context_shards(after(context_keys, value_split), context_values, context_gain, width, "enc", n_enc)
    context = [swap(x, "enc", n_enc, k) if k else x for k, x in enumerate(context)]
    sums = square_sums(after(queries, value_split), self_keys)
    totals = [sums]
    bit = 1
    while bit < n_enc:
        if len(totals) > 1:
            totals = [totals[0] + totals[1]]
        totals = [totals[0], swap(totals[0], "enc", n_enc, bit)]
        bit *= 2
    cosine, sine = rope_tables(after(positions, value_split))
    key_pieces = normed_turned(
        self_keys, 1, totals, key_gain, cosine, sine, full_width, "col", parts, True
    )
    context = jnp.concatenate(context, axis=1)
    others = [0]
    for bit in row_bits:
        others += [k ^ bit for k in others]
    context = [after(swap(context, "row", n_row, k), key_pieces[0]) if k else context for k in others]
    context = jnp.concatenate(context, axis=1)
    key_pieces = [swap(x, "col", n_col, k) if k else x for k, x in enumerate(key_pieces)]

    image_out, *grads = image_attention(
        queries, totals, query_gain, full_width, context, image_cotangent, own_count, n_enc
    )

    values_here = after(values_here, context).reshape(parts * rows, width // parts)
    all_values = [values_here]
    if parts > 1:
        all_values += [swap(values_here, "row", n_row, row_bits[0])]
    grad, sent = halves([swap(x, "enc", n_enc, k) if k else x for k, x in enumerate(grads)])
    query_here = normed_turned(
        after(queries, values_here), 0, totals, query_gain, cosine, sine, full_width, "col", parts, True
    )
    key_pieces = [
        key_pieces[0], *(after(x, all_values[-1], *query_here) for x in key_pieces[1:])
    ]
    keys_here = join_rows(key_pieces, "col")
    got = keys_here
    if parts > 1:
        keys_there = swap(keys_here, "row", n_row, row_bits[0])
        moved = {k: swap(query_here[k], "col", n_col, k) for k in reversed(range(1, parts))}
        query_here = [query_here[0]] + [moved[k] for k in range(1, parts)]
        all_values += [swap(x, "row", n_row, row_bits[1]) for x in all_values]
        all_keys = [keys_here, keys_there, swap(keys_here, "row", n_row, row_bits[1])]
    else:
        all_keys = [lax.all_gather(keys_here, ("row", "col"), axis=0, tiled=True)]
        all_values = [lax.all_gather(values_here, ("row", "col"), axis=0, tiled=True)]

    for i in range(len(row_bits)):
        if i + 1 < len(row_bits):
            grad, sent = split_sum(grad, swap(sent, "row", n_row, 1 << i), 2)
        else:
            grad = split_sum(grad, swap(after(sent, got), "row", n_row, 1 << i), 1)[0]
    if parts > 1:
        keys_there = after(keys_there, grad, *query_here)
        all_keys += [swap(keys_there, "row", n_row, row_bits[1])]

    if parts > 1:
        all_keys = all_keys[::-1]
        all_values = all_values[::-1]

    mixed = [None] * parts
    col_bits = [1 << i for i in reversed(range(n_col.bit_length() - 1))]
    for bit in col_bits[:-2]:
        grad = split_sum(grad, swap(grad, "col", n_col, bit), 1)[0]
    steps = col_bits[-2:]
    got = swap(grad, "col", n_col, steps[0])
    for i, k in enumerate(reversed(range(parts))):
        piece = attention(query_here[k], all_keys, all_values)
        mixed[k] = swap(piece, "col", n_col, k) if k else piece
        if i == 0:
            got = after(got, piece)
    if len(steps) > 1:
        grad = split_sum(grad, got, 1)[0]
        got = swap(grad, "col", n_col, steps[1])
    self_out = join_columns(mixed, "col") if parts > 1 else mixed[0]
    got = after(got, self_out)
    grad_keys_in, grad_values_in = context_gradients(context_keys, context_gain, grad, got, "enc")

    return (self_out, image_out, grad_keys_in, grad_values_in)


def solution(mesh):
    sizes = tuple(mesh.shape[a] for a in ("enc", "row", "col"))
    return jax.shard_map(
        functools.partial(per_device, sizes),
        mesh=mesh,
        in_specs=(
            P(("row", "col"), "enc"),
            P(("row", "col"), "enc"),
            P(("row", "col"), "enc"),
            P(("row", "col"), None),
            P("enc"),
            P("enc"),
            P(("enc", "row"), None),
            P(("enc", "row"), None),
            P(),
            P(("row", "col"), "enc"),
        ),
        out_specs=(
            P(("row", "col"), "enc"),
            P(("row", "col"), "enc"),
            P(("enc", "row"), None),
            P(("enc", "row"), None),
        ),
        check_vma=False,
    )
```
